128 devices in a mesh: sec: 2 (over core), req: 16 (over z, y), kv: 4 (over x).
Axes of the slice: x: 4, y: 4, z: 4, core: 2. Of those that a mesh axis runs over, the one named last changes fastest.
Arguments:
- queries: bfloat16 [2048, 4096], P('req', ('kv', 'sec')), may hold values from -21 to 21
- key_cache: bfloat16 [2048, 4, 32, 128], P('req', 'kv'), may hold values from -21 to 21
- value_cache: bfloat16 [2048, 4, 32, 128], P('req', 'kv'), may hold values from -18 to 18
- new_keys: bfloat16 [2048, 4, 128], P('req', 'kv'), may hold values from -5 to 5
- new_values: bfloat16 [2048, 4, 128], P('req', 'kv'), may hold values from -18 to 18
- lengths: int32 [2048], P('req'), may hold values from 2 to 32
- out_proj: bfloat16 [4096, 4096], P(('kv', 'sec')), may hold values from -0.09375 to 0.09375
- residual: bfloat16 [2048, 4096], P(('req', 'sec', 'kv')), may hold values from -36 to 36
- norm_gain: float32 [4096], replicated, may hold values from 0.1 to 1.9
- expert_ids: int32 [2048, 8], P(('req', 'sec', 'kv')), may hold values from 0 to 127, as said below
- expert_slots: int32 [2048, 8], P(('req', 'sec', 'kv')), may hold values from 0 to 1, as said below
- gate_probs: float32 [2048, 8], P(('req', 'sec', 'kv')), may hold values from 0.1 to 0.4
- w_gate: bfloat16 [128, 4096, 768], P(('sec', 'req', 'kv')), may hold values from -0.09375 to 0.09375
- w_up: bfloat16 [128, 4096, 768], P(('sec', 'req', 'kv')), may hold values from -0.09375 to 0.09375
- w_down: bfloat16 [128, 768, 4096], P(('sec', 'req', 'kv')), may hold values from -0.21875 to 0.21875
Outputs:
- stream: bfloat16 [2048, 4096], P(('req', 'sec', 'kv'))
- moe_out: bfloat16 [2048, 4096], P(('req', 'sec', 'kv'))
The draws below stay inside these ranges and needn't reach their ends.
Inputs may be any that keep to these rules, and one draw needn't show every extreme that they name: `expert_ids`: each row names 8 different experts. In each block of 16 consecutive rows (the rows of one device) every expert is named at least 0 and at most 2 times, and one expert, the same for all blocks, exactly 2 times. `expert_slots`: within a block the entries naming one expert hold different slots, numbered from 0 in row order.
All inputs are finite; a program needn't handle non-finite values.
Results may differ from the reference program's by a relative error of at most 0.029.
Values may be sent and summed in bfloat16 or wider, within the bound.
No kernel may reach another device: no remote copies, remote signals or barrier semaphores. Data moves between devices by JAX's collectives and lax.ppermute only.
A program may use at most 128 MiB of HBM per device.

```python
import jax
import jax.numpy as jnp
from jax import lax

D = 4096
HD = 128
QH = 32
KVH = 4
FFW = 768
TOPK = 8
CTX = 32
TOKENS = 2048
EXPERTS = 128
BLOCK = 16
ROUNDS = 1
CAP = 2


def cache_base(key):
    return jnp.clip(jax.random.normal(key, (TOKENS, KVH, CTX, HD), jnp.float32), -4.0, 4.0)


def route_tables(key):
    block_total = TOKENS // BLOCK
    hot_expert = jax.random.randint(jax.random.fold_in(key, 7001), (), 0, EXPERTS)
    extras = jax.random.randint(jax.random.fold_in(key, 7002), (block_total,), 1, EXPERTS // 2 + 1)
    full_block = jax.random.randint(jax.random.fold_in(key, 7003), (), 0, block_total)
    extras = jnp.where(jnp.arange(block_total) == full_block, EXPERTS // 2, extras).astype(jnp.int32)

    def one_block(block_number, extra):
        block_key = jax.random.fold_in(key, block_number)
        order = jax.random.permutation(jax.random.fold_in(block_key, 1), EXPERTS).astype(jnp.int32)
        position_hot = jnp.argmax(order == hot_expert)
        order = order.at[position_hot].set(order[0]).at[0].set(hot_expert)
        rank = jnp.arange(EXPERTS, dtype=jnp.int32)
        counts = ROUNDS + (rank < extra).astype(jnp.int32) - ((rank >= extra) & (rank < 2 * extra)).astype(jnp.int32)
        ends = jnp.cumsum(counts)
        flat = jnp.arange(BLOCK * TOPK, dtype=jnp.int32)
        which = jnp.sum((ends[None, :] <= flat[:, None]).astype(jnp.int32), axis=1)
        entries = order[which]
        grid = entries.reshape(TOPK, BLOCK).T
        row_order = jax.random.permutation(jax.random.fold_in(block_key, 2), BLOCK)
        grid = grid[row_order]
        column_order = jax.vmap(lambda row_number: jax.random.permutation(jax.random.fold_in(block_key, 100 + row_number), TOPK))(jnp.arange(BLOCK))
        grid = jnp.take_along_axis(grid, column_order, axis=1)
        listed = grid.reshape(-1)
        one_hot = (listed[:, None] == jnp.arange(EXPERTS, dtype=jnp.int32)[None, :]).astype(jnp.int32)
        earlier = jnp.cumsum(one_hot, axis=0) - one_hot
        slot_numbers = jnp.sum(earlier * one_hot, axis=1)
        return (grid, slot_numbers.reshape(BLOCK, TOPK))
    ids_table, slot_table = jax.vmap(one_block)(jnp.arange(block_total), extras)
    return (ids_table.reshape(TOKENS, TOPK).astype(jnp.int32), slot_table.reshape(TOKENS, TOPK).astype(jnp.int32))


def draw_expert_ids(key, part):
    ids_table, slot_table = route_tables(key)
    return ids_table


def draw_expert_slots(key, part):
    ids_table, slot_table = route_tables(key)
    return slot_table


def draw_key_cache(key, part):
    shared = cache_base(key)
    return shared.astype(jnp.bfloat16)


def draw_queries(key, part):
    key = jax.random.fold_in(key, 41)
    drawn = jnp.clip(jax.random.normal(key, (TOKENS, QH * HD), jnp.float32), -4.0, 4.0)
    return drawn.astype(jnp.bfloat16)


def draw_residual(key, part):
    key = jax.random.fold_in(key, 51)
    base_key, row_key, column_key = jax.random.split(key, 3)
    base = jnp.clip(jax.random.normal(base_key, (TOKENS, D), jnp.float32), -4.0, 4.0)
    low_end = jnp.log(0.3)
    high_end = jnp.log(3.0)
    row_scale = jnp.exp(jax.random.uniform(row_key, (TOKENS, 1), jnp.float32, low_end, high_end))
    column_scale = jnp.exp(jax.random.uniform(column_key, (1, D), jnp.float32, low_end, high_end))
    return (base * row_scale * column_scale).astype(jnp.bfloat16)


def plant(array, key, smallest, high):
    index_at = [jax.random.randint(jax.random.fold_in(key, axis), (), 0, length) for axis, length in enumerate(array.shape)]
    main_axis = array.shape.index(max(array.shape))
    next_to = index_at[:main_axis] + [(index_at[main_axis] + 1) % array.shape[main_axis]] + index_at[main_axis + 1:]
    return array.at[tuple(index_at)].set(smallest).at[tuple(next_to)].set(high)


def block_levels(key, dims, pieces, low, largest):
    loudness = 1.0
    for dim, shards_of in pieces:
        draws = jax.random.uniform(jax.random.fold_in(jax.random.fold_in(key, 6), dim), (shards_of,), jnp.float32, low / len(pieces), largest / len(pieces))
        loudness = loudness * jnp.repeat(jnp.exp(draws), dims[dim] // shards_of).reshape((-1,) + (1,) * (len(dims) - 1 - dim))
    return loudness


def bell_draw(own_key, dims, scale, most, shards=(), kind=jnp.bfloat16):
    level = block_levels(own_key, dims, shards, -0.22, 0.18) if shards else 1.0
    values = jax.random.normal(own_key, dims, jnp.float32) * scale * level
    return jnp.minimum(jnp.maximum(values, -most), most).astype(kind)


def setup_inputs(seed: int = 0) -> dict:
    arg_keys = jax.random.split(jax.random.key(seed), 16)
    queries = draw_queries(jax.random.fold_in(arg_keys[15], 71), 0)
    key_cache = draw_key_cache(jax.random.fold_in(arg_keys[15], 71), 0)
    value_cache = bell_draw(arg_keys[2], (TOKENS, KVH, CTX, HD), 3.0, 18.0, ((0, 16), (1, 4)))
    new_keys = bell_draw(arg_keys[3], (TOKENS, KVH, HD), 1.0, 5.0, ((0, 16), (1, 4)))
    new_values = bell_draw(arg_keys[4], (TOKENS, KVH, HD), 3.0, 18.0, ((0, 16), (1, 4)))
    lengths = plant(jax.random.randint(arg_keys[5], (TOKENS,), 2, CTX + 1), jax.random.fold_in(arg_keys[5], 1), 2, CTX).astype(jnp.int32)
    out_proj = bell_draw(arg_keys[6], (QH * HD, D), (QH * HD) ** -0.5, 0.09375, ((0, 8),))
    residual = draw_residual(jax.random.fold_in(arg_keys[15], 71), 0)
    norm_gain = jnp.clip(1.0 + 0.18 * jax.random.normal(arg_keys[8], (D,), jnp.float32), 0.1, 1.9)
    expert_ids = draw_expert_ids(jax.random.fold_in(arg_keys[15], 71), 0)
    expert_slots = draw_expert_slots(jax.random.fold_in(arg_keys[15], 71), 0)
    gate_probs = jnp.clip(0.1 + 0.3 * jax.random.uniform(arg_keys[11], (TOKENS, TOPK), jnp.float32) ** block_levels(arg_keys[11], (TOKENS, TOPK), ((0, 128),), -0.2, 0.2), 0.1, 0.4)
    w_gate = bell_draw(arg_keys[12], (EXPERTS, D, FFW), D ** -0.5, 0.09375, ((0, 128),))
    w_up = bell_draw(arg_keys[13], (EXPERTS, D, FFW), D ** -0.5, 0.09375, ((0, 128),))
    w_down = bell_draw(arg_keys[14], (EXPERTS, FFW, D), FFW ** -0.5, 0.21875, ((0, 128),))
    return {"queries": queries, "key_cache": key_cache, "value_cache": value_cache, "new_keys": new_keys, "new_values": new_values, "lengths": lengths, "out_proj": out_proj, "residual": residual, "norm_gain": norm_gain, "expert_ids": expert_ids, "expert_slots": expert_slots, "gate_probs": gate_probs, "w_gate": w_gate, "w_up": w_up, "w_down": w_down}


def run_expert(operands):
    rows_in, gate_weight, up_weight, down_weight = operands
    gate_out = jnp.dot(rows_in, gate_weight, preferred_element_type=jnp.float32)
    up_out = jnp.dot(rows_in, up_weight, preferred_element_type=jnp.float32)
    hidden = (jax.nn.silu(gate_out) * up_out).astype(jnp.bfloat16)
    return jnp.dot(hidden, down_weight, preferred_element_type=jnp.float32).astype(jnp.bfloat16)

def reference(queries, key_cache, value_cache, new_keys, new_values, lengths, out_proj, residual, norm_gain, expert_ids, expert_slots, gate_probs, w_gate, w_up, w_down):
    group = QH // KVH
    score_scale = 1.0 / HD ** 0.5
    query_heads = queries.astype(jnp.float32).reshape(TOKENS, KVH, group, HD)
    score = jnp.einsum('tghd,tgpd->tghp', query_heads, key_cache.astype(jnp.float32)) * score_scale
    own_score = jnp.einsum('tghd,tgd->tgh', query_heads, new_keys.astype(jnp.float32)) * score_scale
    valid = jnp.arange(CTX, dtype=jnp.int32)[None, :] < lengths[:, None]
    score = jnp.where(valid[:, None, None, :], score, -jnp.inf)
    highest = jnp.maximum(lax.optimization_barrier(jnp.max(score, axis=-1)), own_score)
    raised = jnp.exp(score - highest[..., None])
    own_raised = jnp.exp(own_score - highest)
    denominator = lax.optimization_barrier(jnp.sum(raised, axis=-1)) + own_raised
    weight = (raised / denominator[..., None]).astype(jnp.bfloat16)
    own_weight = (own_raised / denominator).astype(jnp.bfloat16)
    attn = jnp.einsum('tghp,tgpd->tghd', weight.astype(jnp.float32), value_cache.astype(jnp.float32))
    attn = attn + own_weight.astype(jnp.float32)[..., None] * new_values.astype(jnp.float32)[:, :, None, :]
    attn = attn.astype(jnp.bfloat16).reshape(TOKENS, QH * HD)
    proj = jnp.dot(attn, out_proj, preferred_element_type=jnp.float32)
    stream = (residual.astype(jnp.float32) + proj).astype(jnp.bfloat16)
    widened = lax.optimization_barrier(stream).astype(jnp.float32)
    mean_square = lax.optimization_barrier(jnp.mean(widened * widened, axis=-1, keepdims=True))
    normed = (widened * lax.rsqrt(mean_square + 1e-06) * norm_gain).astype(jnp.bfloat16)
    block_count = TOKENS // BLOCK
    block_of = (jnp.arange(TOKENS, dtype=jnp.int32) // BLOCK)[:, None]
    slot_index = (expert_ids * (block_count * CAP) + block_of * CAP + expert_slots).astype(jnp.int32).reshape(-1)
    repeated = jnp.broadcast_to(normed[:, None, :], (TOKENS, TOPK, D)).reshape(TOKENS * TOPK, D)
    expert_in = jnp.zeros((EXPERTS * block_count * CAP, D), jnp.bfloat16).at[slot_index].set(repeated)
    expert_in = expert_in.reshape(EXPERTS, block_count * CAP, D)
    expert_out = lax.map(run_expert, (expert_in, w_gate, w_up, w_down))
    picked = expert_out.reshape(EXPERTS * block_count * CAP, D)[slot_index].reshape(TOKENS, TOPK, D)
    moe_out = lax.optimization_barrier(jnp.sum(picked.astype(jnp.float32) * gate_probs[..., None], axis=1)).astype(jnp.bfloat16)
    return (stream, moe_out)
```

```python
import jax
import jax.numpy as jnp
from jax import lax
from jax.experimental import pallas as pl
from jax.experimental.pallas import tpu as pltpu
from jax.sharding import PartitionSpec as P

LANES = 128
F32 = jnp.float32
BF16 = jnp.bfloat16
MIB = 1 << 20

VMEM = pltpu.VMEM
SMEM = pltpu.SMEM


def whole(space=VMEM):
    return pl.BlockSpec(memory_space=space)


def attend_kernel(sec_ref, q_ref, kc_ref, vc_ref, nk_ref, nv_ref, len_ref, wo_ref, theirs_ref, mine_ref, attn_ref):
    rows, head_width = q_ref.shape
    heads = head_width // LANES
    positions = kc_ref.shape[0] // rows
    group = 16
    scale = 1.0 / LANES**0.5
    half = rows // 2

    @pl.when(pl.program_id(0) == 0)
    def _():
        r = lax.broadcasted_iota(jnp.int32, (rows, rows), 0)
        c = lax.broadcasted_iota(jnp.int32, (rows, rows), 1)
        lengths = jnp.sum(jnp.where(r == c, len_ref[...], 0).astype(F32), axis=1, keepdims=True)
        span = group * positions
        row_token = lax.broadcasted_iota(jnp.int32, (heads * group, span), 0) % group
        column = lax.broadcasted_iota(jnp.int32, (heads * group, span), 1)
        own_column = column - row_token * positions
        own_position = jnp.where(own_column >= 0, own_column, positions).astype(F32)
        for g in range(rows // group):
            at = pl.ds(g * group, group)
            q = jnp.concatenate([q_ref[at, pl.ds(h * LANES, LANES)] for h in range(heads)], axis=0)
            keys = kc_ref[pl.ds(g * span, span), :]
            score = lax.dot_general(q, keys, (((1,), (1,)), ((), ())), preferred_element_type=F32) * scale
            new_key = jnp.concatenate([nk_ref[at, :].astype(F32)] * heads, axis=0)
            own_score = jnp.sum(q.astype(F32) * new_key, axis=1, keepdims=True) * scale
            limit = jnp.concatenate([lengths[g * group : (g + 1) * group]] * heads, axis=0)
            score = jnp.where(own_position < limit, score, -jnp.inf)
            highest = jnp.maximum(jnp.max(score, axis=1, keepdims=True), own_score)
            raised = jnp.exp(score - highest)
            own_raised = jnp.exp(own_score - highest)
            inverse = 1.0 / (jnp.sum(raised, axis=1, keepdims=True) + own_raised)
            weight = (raised * inverse).astype(BF16)
            own_weight = (own_raised * inverse).astype(BF16).astype(F32)
            values = vc_ref[pl.ds(g * span, span), :]
            out = jnp.dot(weight, values, preferred_element_type=F32)
            out = out + own_weight * jnp.concatenate([nv_ref[at, :].astype(F32)] * heads, axis=0)
            out = out.astype(BF16)
            place = lax.rem(g * group + half * (1 - sec_ref[0]), rows)
            place = pl.multiple_of(place, group)
            for h in range(heads):
                attn_ref[pl.ds(place, group), pl.ds(h * LANES, LANES)] = out[h * group : (h + 1) * group]

    proj = jnp.dot(attn_ref[...], wo_ref[...], preferred_element_type=F32)
    theirs_ref[...] = proj[:half].astype(BF16)
    mine_ref[...] = proj[half:].astype(BF16)


def attend(sec, q, kc, vc, nk, nv, lengths, wo):
    rows, head_width = q.shape
    width = wo.shape[1]
    steps = 4
    block = width // steps
    full = lambda a: pl.BlockSpec(a.shape, lambda i, s: (0, 0))
    out = jax.ShapeDtypeStruct((rows // 2, width), BF16)
    out_spec = pl.BlockSpec((rows // 2, block), lambda i, s: (0, i))
    return pl.pallas_call(
        attend_kernel,
        grid_spec=pltpu.PrefetchScalarGridSpec(
            num_scalar_prefetch=1,
            grid=(steps,),
            in_specs=[full(a) for a in (q, kc, vc, nk, nv, lengths)] + [pl.BlockSpec((head_width, block), lambda i, s: (0, i))],
            out_specs=[out_spec, out_spec],
            scratch_shapes=[pltpu.VMEM((rows, head_width), BF16)],
        ),
        out_shape=[out, out],
        compiler_params=pltpu.CompilerParams(vmem_limit_bytes=24 * MIB),
        name="attend",
    )(sec, q, kc, vc, nk, nv, lengths, wo)


def quarter_kernel(kv_ref, mine_ref, got_ref, *out_refs):
    count = len(out_refs)
    rows = mine_ref.shape[0] // count
    for step, out_ref in enumerate(out_refs):
        at = pl.ds(pl.multiple_of(lax.rem(kv_ref[0] + step, count) * rows, rows), rows)
        out_ref[...] = (mine_ref[at, :].astype(F32) + got_ref[at, :].astype(F32)).astype(BF16)


def quarter(kv, mine, got, count):
    rows, width = mine.shape
    out = jax.ShapeDtypeStruct((rows // count, width), BF16)
    return pl.pallas_call(
        quarter_kernel,
        in_specs=[whole(SMEM), whole(), whole()],
        out_specs=[whole()] * count,
        out_shape=[out] * count,
        name="quarter",
    )(kv, mine, got)


def route_kernel(ids_ref, slots_ref, *refs):
    part_refs, (residual_ref, gain_ref, stream_ref, out_ref, wide_ref, row_ref) = refs[:-6], refs[-6:]
    rows, width = residual_ref.shape
    pieces = width // LANES
    top = ids_ref.shape[0]
    capacity = out_ref.shape[1]
    out_ref[...] = jnp.zeros_like(out_ref)
    proj = part_refs[0][...].astype(F32)
    for part_ref in part_refs[1:]:
        proj = proj + part_ref[...].astype(F32)
    stream = (residual_ref[...].astype(F32) + proj).astype(BF16)
    stream_ref[...] = stream
    widened = stream.astype(F32)
    mean_square = jnp.mean(widened * widened, axis=-1, keepdims=True)
    normed = widened * lax.rsqrt(mean_square + 1e-06) * gain_ref[...]
    for t in range(0, rows, 8):
        for s in range(pieces):
            wide_ref[pl.ds(t * pieces + s, 8, stride=pieces), :] = normed[t : t + 8, s * LANES : (s + 1) * LANES]
    row_ref[...] = wide_ref[...].astype(BF16).reshape(rows, pieces, LANES)

    def one(t, carry):
        row = row_ref[t]
        for k in range(top):
            out_ref[ids_ref[k, t], slots_ref[k, t]] = row
        return carry

    lax.fori_loop(0, rows, one, 0)


def route(ids, slots, parts, residual, gain, expert_count, capacity):
    rows, width = residual.shape
    pieces = width // LANES
    return pl.pallas_call(
        route_kernel,
        in_specs=[whole(SMEM), whole(SMEM)] + [whole()] * (len(parts) + 2),
        out_specs=[whole(), whole()],
        out_shape=[
            jax.ShapeDtypeStruct((rows, width), BF16),
            jax.ShapeDtypeStruct((expert_count, capacity, pieces, LANES), BF16),
        ],
        scratch_shapes=[pltpu.VMEM((rows * pieces, LANES), F32), pltpu.VMEM((rows, pieces, LANES), BF16)],
        compiler_params=pltpu.CompilerParams(vmem_limit_bytes=16 * MIB),
        name="route",
    )(ids, slots, *parts, residual, gain)


def expert_kernel(x_ref, wg_ref, wu_ref, wd_ref, out_ref, wide_ref, flat_ref, wg, wu, wd, hidden_ref, in_sems, down_sems):
    rows, pieces, _ = x_ref.shape
    hidden_width = wg_ref.shape[1]
    width = pieces * LANES
    ncols = 256
    nsteps = hidden_width // ncols
    dsteps = down_sems.shape[0]
    dcols = width // dsteps

    def gate_copies(n):
        at = pl.ds(n * ncols, ncols)
        return (
            pltpu.make_async_copy(wg_ref.at[:, at], wg.at[n], in_sems.at[0, n]),
            pltpu.make_async_copy(wu_ref.at[:, at], wu.at[n], in_sems.at[1, n]),
        )

    def down_copy(n):
        return pltpu.make_async_copy(wd_ref.at[:, pl.ds(n * dcols, dcols)], wd.at[n], down_sems.at[n])

    for n in range(nsteps):
        for copy in gate_copies(n):
            copy.start()
    for n in range(dsteps):
        down_copy(n).start()

    group = 16

    def spread(i, carry):
        base = pl.multiple_of(i * group, group)
        wide_ref[pl.ds(0, group * pieces), :] = x_ref[pl.ds(base, group)].reshape(group * pieces, LANES).astype(F32)
        for s in range(pieces):
            low = wide_ref[pl.ds(s, 8, stride=pieces), :]
            high = wide_ref[pl.ds(8 * pieces + s, 8, stride=pieces), :]
            flat_ref[pl.ds(base, group), pl.ds(s * LANES, LANES)] = jnp.concatenate([low, high], axis=0).astype(BF16)
        return carry

    lax.fori_loop(0, rows // group, spread, 0)

    for n in range(nsteps):
        for copy in gate_copies(n):
            copy.wait()
        gate = jnp.dot(flat_ref[...], wg[n], preferred_element_type=F32)
        up = jnp.dot(flat_ref[...], wu[n], preferred_element_type=F32)
        hidden_ref[:, pl.ds(n * ncols, ncols)] = (gate / (1.0 + jnp.exp(-gate)) * up).astype(BF16)

    for n in range(dsteps):
        down_copy(n).wait()
        done = jnp.dot(hidden_ref[...], wd[n], preferred_element_type=F32)
        for r in range(0, rows, 8):
            for s in range(dcols // LANES):
                wide_ref[pl.ds(r * pieces + n * (dcols // LANES) + s, 8, stride=pieces), :] = done[
                    r : r + 8, s * LANES : (s + 1) * LANES
                ]

    def narrow(i, carry):
        base = pl.multiple_of(i * group, group)
        at = pl.ds(pl.multiple_of(i * group * pieces, group * pieces), group * pieces)
        out_ref[pl.ds(base, group)] = wide_ref[at, :].astype(BF16).reshape(group, pieces, LANES)
        return carry

    lax.fori_loop(0, rows // group, narrow, 0)


def expert(x, wg, wu, wd):
    rows, pieces, _ = x.shape
    width, hidden_width = wg.shape
    nsteps, dsteps = hidden_width // 256, 4
    return pl.pallas_call(
        expert_kernel,
        in_specs=[whole()] + [pl.BlockSpec(memory_space=pl.ANY)] * 3,
        out_specs=whole(),
        out_shape=jax.ShapeDtypeStruct(x.shape, BF16),
        scratch_shapes=[
            pltpu.VMEM((rows * pieces, LANES), F32),
            pltpu.VMEM((rows, width), BF16),
            pltpu.VMEM((nsteps, width, 256), BF16),
            pltpu.VMEM((nsteps, width, 256), BF16),
            pltpu.VMEM((dsteps, hidden_width, width // dsteps), BF16),
            pltpu.VMEM((rows, hidden_width), BF16),
            pltpu.SemaphoreType.DMA((2, nsteps)),
            pltpu.SemaphoreType.DMA((dsteps,)),
        ],
        compiler_params=pltpu.CompilerParams(vmem_limit_bytes=44 * MIB),
        name="expert",
    )(x, wg, wu, wd)


def combine_kernel(ids_ref, slots_ref, probs_ref, rows_ref, out_ref, wide_ref):
    rows, width = out_ref.shape
    pieces = width // LANES
    top = ids_ref.shape[0]

    def one(t, carry):
        total = None
        for k in range(top):
            term = rows_ref[ids_ref[k, t], slots_ref[k, t]].astype(F32) * probs_ref[k, t]
            total = term if total is None else total + term
        wide_ref[pl.ds(pl.multiple_of(t * pieces, pieces), pieces), :] = total
        return carry

    lax.fori_loop(0, rows, one, 0)
    for s in range(pieces):
        low = wide_ref[pl.ds(s, 8, stride=pieces), :]
        high = wide_ref[pl.ds(8 * pieces + s, 8, stride=pieces), :]
        out_ref[:, pl.ds(s * LANES, LANES)] = jnp.concatenate([low, high], axis=0).astype(BF16)


def combine(ids, slots, probs, returned, width):
    rows = ids.shape[1]
    return pl.pallas_call(
        combine_kernel,
        in_specs=[whole(SMEM)] * 3 + [whole()],
        out_specs=whole(),
        out_shape=jax.ShapeDtypeStruct((rows, width), BF16),
        scratch_shapes=[pltpu.VMEM((rows * width // LANES, LANES), F32)],
        compiler_params=pltpu.CompilerParams(vmem_limit_bytes=16 * MIB),
        name="combine",
    )(ids, slots, probs, returned)


def on_device(
    queries,
    key_cache,
    value_cache,
    new_keys,
    new_values,
    lengths,
    out_proj,
    residual,
    norm_gain,
    expert_ids,
    expert_slots,
    gate_probs,
    w_gate,
    w_up,
    w_down,
):
    row_count = queries.shape[0]
    width = out_proj.shape[1]
    pieces = width // LANES
    sec_count, group_count = lax.axis_size("sec"), lax.axis_size("kv")
    expert_count = sec_count * lax.axis_size("req") * group_count
    row_share, top_count = expert_ids.shape
    capacity = top_count * row_share // expert_count + 1
    sec = lax.axis_index("sec").astype(jnp.int32).reshape(1)
    kv = lax.axis_index("kv").astype(jnp.int32).reshape(1)

    theirs, mine = attend(
        sec,
        queries,
        key_cache.reshape(-1, LANES),
        value_cache.reshape(-1, LANES),
        new_keys.reshape(row_count, LANES),
        new_values.reshape(row_count, LANES),
        lengths.reshape(1, row_count),
        out_proj,
    )
    got = lax.ppermute(theirs, "sec", [(i, 1 - i) for i in range(sec_count)])
    quarters = quarter(kv, mine, got, group_count)
    parts = [quarters[0]] + [
        lax.ppermute(quarters[s], "kv", [(i, (i + s) % group_count) for i in range(group_count)])
        for s in range(1, group_count)
    ]
    ids, slots, probs = expert_ids.T, expert_slots.T, gate_probs.T
    stream, outgoing = route(ids, slots, parts, residual, norm_gain.reshape(1, width), expert_count, capacity)

    def exchange(rows):
        sent = rows.reshape(expert_count, capacity * pieces, LANES)
        return lax.all_to_all(sent, ("sec", "req", "kv"), split_axis=0, concat_axis=0, tiled=True)

    arrived = exchange(outgoing).reshape(expert_count * capacity, pieces, LANES)
    finished = expert(arrived, w_gate[0], w_up[0], w_down[0])
    returned = exchange(finished).reshape(expert_count, capacity, pieces, LANES)
    moe_out = combine(ids, slots, probs, returned, width)
    return (stream, moe_out)


def solution(mesh):
    return jax.shard_map(
        on_device,
        mesh=mesh,
        in_specs=(
            P("req", ("kv", "sec")),
            P("req", "kv", None, None),
            P("req", "kv", None, None),
            P("req", "kv", None),
            P("req", "kv", None),
            P("req"),
            P(("kv", "sec"), None),
            P(("req", "sec", "kv"), None),
            P(),
            P(("req", "sec", "kv"), None),
            P(("req", "sec", "kv"), None),
            P(("req", "sec", "kv"), None),
            P(("sec", "req", "kv"), None, None),
            P(("sec", "req", "kv"), None, None),
            P(("sec", "req", "kv"), None, None),
        ),
        out_specs=(P(("req", "sec", "kv"), None), P(("req", "sec", "kv"), None)),
        check_vma=False,
    )
```

```python
import jax
import jax.numpy as jnp
from jax import lax
from jax.experimental import pallas as pl
from jax.experimental.pallas import tpu as pltpu
from jax.sharding import PartitionSpec as P

LANES = 128
F32 = jnp.float32
BF16 = jnp.bfloat16
MIB = 1 << 20

GAP = 1

VMEM = pltpu.VMEM
SMEM = pltpu.SMEM


def whole(space=VMEM):
    return pl.BlockSpec(memory_space=space)


PROJ_STEPS = 4
CACHE_STEPS = 4


def attend_kernel(
    sec_ref,
    len_ref,
    q_hbm,
    kc_hbm,
    vc_hbm,
    nk_hbm,
    nv_hbm,
    wo_hbm,
    theirs_ref,
    mine_ref,
    q_ref,
    kc_ref,
    vc_ref,
    nk_ref,
    nv_ref,
    wo_ref,
    attn_ref,
    small_sems,
    key_sems,
    value_sems,
    wo_sems,
):
    rows, head_width = q_ref.shape
    heads = head_width // LANES
    positions = kc_ref.shape[0] // rows
    group = 16
    scale = 1.0 / LANES**0.5
    half = rows // 2
    block = wo_ref.shape[2]
    cache_rows = kc_ref.shape[0] // CACHE_STEPS

    small = [
        pltpu.make_async_copy(source, target, small_sems.at[i])
        for i, (source, target) in enumerate(((q_hbm, q_ref), (nk_hbm, nk_ref), (nv_hbm, nv_ref)))
    ]
    part = [pl.ds(i * cache_rows, cache_rows) for i in range(CACHE_STEPS)]
    key_copies = [pltpu.make_async_copy(kc_hbm.at[at], kc_ref.at[at], key_sems.at[i]) for i, at in enumerate(part)]
    value_copies = [pltpu.make_async_copy(vc_hbm.at[at], vc_ref.at[at], value_sems.at[i]) for i, at in enumerate(part)]
    wo_copies = [
        pltpu.make_async_copy(wo_hbm.at[:, pl.ds(i * block, block)], wo_ref.at[i], wo_sems.at[i])
        for i in range(PROJ_STEPS)
    ]
    for copy in small:
        copy.start()
    for i in range(CACHE_STEPS):
        key_copies[i].start()
        value_copies[i].start()
    for copy in wo_copies:
        copy.start()

    r = lax.broadcasted_iota(jnp.int32, (rows, rows), 0)
    c = lax.broadcasted_iota(jnp.int32, (rows, rows), 1)
    lengths = jnp.sum(jnp.where(r == c, len_ref[...], 0).astype(F32), axis=1, keepdims=True)
    span = group * positions
    row_token = lax.broadcasted_iota(jnp.int32, (heads * group, span), 0) % group
    column = lax.broadcasted_iota(jnp.int32, (heads * group, span), 1)
    own_column = column - row_token * positions
    own_position = jnp.where(own_column >= 0, own_column, positions).astype(F32)
    for copy in small:
        copy.wait()
    per_step = rows // group // CACHE_STEPS
    for g in range(rows // group):
        if g % per_step == 0:
            key_copies[g // per_step].wait()
            value_copies[g // per_step].wait()
        at = pl.ds(g * group, group)
        q = jnp.concatenate([q_ref[at, pl.ds(h * LANES, LANES)] for h in range(heads)], axis=0)
        keys = kc_ref[pl.ds(g * span, span), :]
        score = lax.dot_general(q, keys, (((1,), (1,)), ((), ())), preferred_element_type=F32) * scale
        new_key = jnp.concatenate([nk_ref[at, :].astype(F32)] * heads, axis=0)
        own_score = jnp.sum(q.astype(F32) * new_key, axis=1, keepdims=True) * scale
        limit = jnp.concatenate([lengths[g * group : (g + 1) * group]] * heads, axis=0)
        score = jnp.where(own_position < limit, score, -jnp.inf)
        highest = jnp.maximum(jnp.max(score, axis=1, keepdims=True), own_score)
        raised = jnp.exp(score - highest)
        own_raised = jnp.exp(own_score - highest)
        inverse = 1.0 / (jnp.sum(raised, axis=1, keepdims=True) + own_raised)
        weight = (raised * inverse).astype(BF16)
        own_weight = (own_raised * inverse).astype(BF16).astype(F32)
        values = vc_ref[pl.ds(g * span, span), :]
        out = jnp.dot(weight, values, preferred_element_type=F32)
        out = out + own_weight * jnp.concatenate([nv_ref[at, :].astype(F32)] * heads, axis=0)
        out = out.astype(BF16)
        place = lax.rem(g * group + half * (1 - sec_ref[0]), rows)
        place = pl.multiple_of(place, group)
        for h in range(heads):
            attn_ref[pl.ds(place, group), pl.ds(h * LANES, LANES)] = out[h * group : (h + 1) * group]

    for i in range(PROJ_STEPS):
        wo_copies[i].wait()
        proj = jnp.dot(attn_ref[...], wo_ref[i], preferred_element_type=F32)
        at = pl.ds(i * block, block)
        theirs_ref[:, at] = proj[:half].astype(BF16)
        mine_ref[:, at] = proj[half:].astype(BF16)


def attend(sec, lengths, q, kc, vc, nk, nv, wo):
    rows, head_width = q.shape
    width = wo.shape[1]
    out = jax.ShapeDtypeStruct((rows // 2, width), BF16)
    far = [pltpu.with_memory_space_constraint(a, pltpu.HBM) for a in (q, kc, vc, nk, nv, wo)]
    return pl.pallas_call(
        attend_kernel,
        in_specs=[whole(SMEM), whole()] + [whole(pltpu.HBM)] * 6,
        out_specs=[whole(), whole()],
        out_shape=[out, out],
        scratch_shapes=[pltpu.VMEM(a.shape, BF16) for a in (q, kc, vc, nk, nv)]
        + [
            pltpu.VMEM((PROJ_STEPS, head_width, width // PROJ_STEPS), BF16),
            pltpu.VMEM((rows, head_width), BF16),
            pltpu.SemaphoreType.DMA((3,)),
            pltpu.SemaphoreType.DMA((CACHE_STEPS,)),
            pltpu.SemaphoreType.DMA((CACHE_STEPS,)),
            pltpu.SemaphoreType.DMA((PROJ_STEPS,)),
        ],
        compiler_params=pltpu.CompilerParams(vmem_limit_bytes=14 * MIB),
        name="attend",
    )(sec, lengths, *far)


def quarter_kernel(kv_ref, mine_ref, got_ref, *out_refs):
    count = len(out_refs)
    rows = mine_ref.shape[0] // count
    for step, out_ref in enumerate(out_refs):
        at = pl.ds(pl.multiple_of(lax.rem(kv_ref[0] + step, count) * rows, rows), rows)
        out_ref[...] = (mine_ref[at, :].astype(F32) + got_ref[at, :].astype(F32)).astype(BF16)


def quarter(kv, mine, got, count):
    rows, width = mine.shape
    out = jax.ShapeDtypeStruct((rows // count, width), BF16)
    return pl.pallas_call(
        quarter_kernel,
        in_specs=[whole(SMEM), whole(), whole()],
        out_specs=[whole()] * count,
        out_shape=[out] * count,
        compiler_params=pltpu.CompilerParams(vmem_limit_bytes=4 * MIB),
        name="quarter",
    )(kv, mine, got)


def route_kernel(ids_ref, slots_ref, *refs):
    part_refs, (residual_ref, gain_ref, stream_ref, out_ref, wide_ref) = refs[:-5], refs[-5:]
    rows, width = residual_ref.shape
    pieces = width // LANES
    top = ids_ref.shape[0]
    stride = pieces + GAP
    out_ref[...] = jnp.zeros_like(out_ref)
    proj = part_refs[0][...].astype(F32)
    for part_ref in part_refs[1:]:
        proj = proj + part_ref[...].astype(F32)
    stream = (residual_ref[...].astype(F32) + proj).astype(BF16)
    stream_ref[...] = stream
    widened = stream.astype(F32)
    mean_square = jnp.mean(widened * widened, axis=-1, keepdims=True)
    normed = widened * lax.rsqrt(mean_square + 1e-06) * gain_ref[...]
    for t in range(0, rows, 8):
        for s in range(pieces):
            wide_ref[pl.ds(t * stride + s, 8, stride=stride), :] = normed[t : t + 8, s * LANES : (s + 1) * LANES]

    def one(t, carry):
        row = wide_ref[pl.ds(t * stride, pieces), :].astype(BF16)
        for k in range(top):
            out_ref[ids_ref[k, t], slots_ref[k, t]] = row
        return carry

    lax.fori_loop(0, rows, one, 0)


def route(ids, slots, parts, residual, gain, expert_count, capacity):
    rows, width = residual.shape
    pieces = width // LANES
    return pl.pallas_call(
        route_kernel,
        in_specs=[whole(SMEM), whole(SMEM)] + [whole()] * (len(parts) + 2),
        out_specs=[whole(), whole()],
        out_shape=[
            jax.ShapeDtypeStruct((rows, width), BF16),
            jax.ShapeDtypeStruct((expert_count, capacity, pieces, LANES), BF16),
        ],
        scratch_shapes=[pltpu.VMEM((rows * (pieces + GAP), LANES), F32)],
        compiler_params=pltpu.CompilerParams(vmem_limit_bytes=4 * MIB),
        name="route",
    )(ids, slots, *parts, residual, gain)


def load_kernel(*refs):
    count = len(refs) // 2
    sems = refs[-1]
    copies = [pltpu.make_async_copy(refs[i], refs[count + i], sems.at[i]) for i in range(count)]
    for copy in copies:
        copy.start()
    for copy in copies:
        copy.wait()


def load(*weights):
    size = sum(w.size * 2 for w in weights)
    return pl.pallas_call(
        load_kernel,
        in_specs=[whole(pltpu.HBM)] * len(weights),
        out_specs=[whole()] * len(weights),
        out_shape=[pltpu.VMEM(w.shape, w.dtype) for w in weights],
        scratch_shapes=[pltpu.SemaphoreType.DMA((len(weights),))],
        compiler_params=pltpu.CompilerParams(vmem_limit_bytes=2 * MIB),
        cost_estimate=pl.CostEstimate(flops=0, bytes_accessed=2 * size, transcendentals=0),
        name="load",
    )(*[pltpu.with_memory_space_constraint(w, pltpu.HBM) for w in weights])


def expert_kernel(x_ref, wg_ref, wu_ref, wd_ref, out_ref, wide_ref, flat_ref, hidden_ref):
    rows, pieces, _ = x_ref.shape
    hidden_width = wg_ref.shape[1]
    width = pieces * LANES
    stride = pieces + GAP
    ncols = 256
    dcols = 1024
    group = 16

    def spread(i, carry):
        base = pl.multiple_of(i * group, group)
        for r in range(group):
            wide_ref[pl.ds(r * stride, pieces), :] = x_ref[base + r].astype(F32)
        for s in range(pieces):
            low = wide_ref[pl.ds(s, 8, stride=stride), :]
            high = wide_ref[pl.ds(8 * stride + s, 8, stride=stride), :]
            flat_ref[pl.ds(base, group), pl.ds(s * LANES, LANES)] = jnp.concatenate([low, high], axis=0).astype(BF16)
        return carry

    lax.fori_loop(0, rows // group, spread, 0)

    for n in range(hidden_width // ncols):
        at = pl.ds(n * ncols, ncols)
        gate = jnp.dot(flat_ref[...], wg_ref[:, at], preferred_element_type=F32)
        up = jnp.dot(flat_ref[...], wu_ref[:, at], preferred_element_type=F32)
        hidden_ref[:, at] = (gate / (1.0 + jnp.exp(-gate)) * up).astype(BF16)

    for n in range(width // dcols):
        done = jnp.dot(hidden_ref[...], wd_ref[:, pl.ds(n * dcols, dcols)], preferred_element_type=F32)
        for r in range(0, rows, 8):
            for s in range(dcols // LANES):
                wide_ref[pl.ds(r * stride + n * (dcols // LANES) + s, 8, stride=stride), :] = done[
                    r : r + 8, s * LANES : (s + 1) * LANES
                ]

    def narrow(i, carry):
        base = pl.multiple_of(i * group, group)
        for r in range(group):
            out_ref[base + r] = wide_ref[pl.ds((base + r) * stride, pieces), :].astype(BF16)
        return carry

    lax.fori_loop(0, rows // group, narrow, 0)


def expert(x, wg, wu, wd):
    rows, pieces, _ = x.shape
    width, hidden_width = wg.shape
    near = [pltpu.with_memory_space_constraint(w, pltpu.VMEM) for w in (wg, wu, wd)]
    return pl.pallas_call(
        expert_kernel,
        in_specs=[whole()] * 4,
        out_specs=whole(),
        out_shape=jax.ShapeDtypeStruct(x.shape, BF16),
        scratch_shapes=[
            pltpu.VMEM((rows * (pieces + GAP), LANES), F32),
            pltpu.VMEM((rows, width), BF16),
            pltpu.VMEM((rows, hidden_width), BF16),
        ],
        compiler_params=pltpu.CompilerParams(vmem_limit_bytes=16 * MIB),
        name="expert",
    )(x, *near)


def combine_kernel(ids_ref, slots_ref, probs_ref, rows_ref, out_ref, wide_ref):
    rows, width = out_ref.shape
    pieces = width // LANES
    top = ids_ref.shape[0]
    stride = pieces + GAP

    def one(t, carry):
        total = None
        for k in range(top):
            term = rows_ref[ids_ref[k, t], slots_ref[k, t]].astype(F32) * probs_ref[k, t]
            total = term if total is None else total + term
        wide_ref[pl.ds(t * stride, pieces), :] = total
        return carry

    lax.fori_loop(0, rows, one, 0)
    for s in range(pieces):
        low = wide_ref[pl.ds(s, 8, stride=stride), :]
        high = wide_ref[pl.ds(8 * stride + s, 8, stride=stride), :]
        out_ref[:, pl.ds(s * LANES, LANES)] = jnp.concatenate([low, high], axis=0).astype(BF16)


def combine(ids, slots, probs, returned, width):
    rows = ids.shape[1]
    return pl.pallas_call(
        combine_kernel,
        in_specs=[whole(SMEM)] * 3 + [whole()],
        out_specs=whole(),
        out_shape=jax.ShapeDtypeStruct((rows, width), BF16),
        scratch_shapes=[pltpu.VMEM((rows * (width // LANES + GAP), LANES), F32)],
        compiler_params=pltpu.CompilerParams(vmem_limit_bytes=4 * MIB),
        name="combine",
    )(ids, slots, probs, returned)


def on_device(
    queries,
    key_cache,
    value_cache,
    new_keys,
    new_values,
    lengths,
    out_proj,
    residual,
    norm_gain,
    expert_ids,
    expert_slots,
    gate_probs,
    w_gate,
    w_up,
    w_down,
):
    row_count = queries.shape[0]
    width = out_proj.shape[1]
    pieces = width // LANES
    sec_count, group_count = lax.axis_size("sec"), lax.axis_size("kv")
    expert_count = sec_count * lax.axis_size("req") * group_count
    row_share, top_count = expert_ids.shape
    capacity = top_count * row_share // expert_count + 1
    sec = lax.axis_index("sec").astype(jnp.int32).reshape(1)
    kv = lax.axis_index("kv").astype(jnp.int32).reshape(1)

    theirs, mine = attend(
        sec,
        lengths.reshape(1, row_count),
        queries,
        key_cache.reshape(-1, LANES),
        value_cache.reshape(-1, LANES),
        new_keys.reshape(row_count, LANES),
        new_values.reshape(row_count, LANES),
        out_proj,
    )
    got = lax.ppermute(theirs, "sec", [(i, 1 - i) for i in range(sec_count)])
    quarters = quarter(kv, mine, got, group_count)
    parts = [quarters[0]] + [
        lax.ppermute(quarters[s], "kv", [(i, (i + s) % group_count) for i in range(group_count)])
        for s in range(1, group_count)
    ]
    ids, slots, probs = expert_ids.T, expert_slots.T, gate_probs.T
    stream, outgoing = route(ids, slots, parts, residual, norm_gain.reshape(1, width), expert_count, capacity)

    def exchange(rows):
        sent = rows.reshape(expert_count, capacity * pieces, LANES)
        return lax.all_to_all(sent, ("sec", "req", "kv"), split_axis=0, concat_axis=0, tiled=True)

    outgoing, *weights = lax.optimization_barrier((outgoing, *load(w_gate[0], w_up[0], w_down[0])))
    arrived = exchange(outgoing).reshape(expert_count * capacity, pieces, LANES)
    finished = expert(arrived, *weights)
    returned = exchange(finished).reshape(expert_count, capacity, pieces, LANES)
    moe_out = combine(ids, slots, probs, returned, width)
    return (stream, moe_out)


def solution(mesh):
    return jax.shard_map(
        on_device,
        mesh=mesh,
        in_specs=(
            P("req", ("kv", "sec")),
            P("req", "kv", None, None),
            P("req", "kv", None, None),
            P("req", "kv", None),
            P("req", "kv", None),
            P("req"),
            P(("kv", "sec"), None),
            P(("req", "sec", "kv"), None),
            P(),
            P(("req", "sec", "kv"), None),
            P(("req", "sec", "kv"), None),
            P(("req", "sec", "kv"), None),
            P(("sec", "req", "kv"), None, None),
            P(("sec", "req", "kv"), None, None),
            P(("sec", "req", "kv"), None, None),
        ),
        out_specs=(P(("req", "sec", "kv"), None), P(("req", "sec", "kv"), None)),
        check_vma=False,
    )
```

```python
import math

import jax
import jax.numpy as jnp
from jax import lax
from jax.experimental import pallas as pl
from jax.experimental.pallas import tpu as pltpu
from jax.sharding import PartitionSpec as P

LANES = 128
F32 = jnp.float32
BF16 = jnp.bfloat16
MIB = 1 << 20

GAP = 1

VMEM = pltpu.VMEM
SMEM = pltpu.SMEM


def whole(space=VMEM):
    return pl.BlockSpec(memory_space=space)


def attend_kernel(
    sec_ref,
    len_hbm,
    q_hbm,
    kc_hbm,
    vc_hbm,
    nk_hbm,
    nv_hbm,
    wo_hbm,
    theirs_ref,
    mine_ref,
    len_ref,
    q_ref,
    kc_ref,
    vc_ref,
    nk_ref,
    nv_ref,
    wo_ref,
    attn_ref,
    sems,
):
    rows, head_width = q_ref.shape
    heads = head_width // LANES
    positions = kc_ref.shape[0] // rows
    group = 8
    to_exponent = math.log2(math.e) / LANES**0.5
    half = rows // 2

    small = [
        pltpu.make_async_copy(source, target, sems.at[i])
        for i, (source, target) in enumerate(((len_hbm, len_ref), (q_hbm, q_ref), (nk_hbm, nk_ref), (nv_hbm, nv_ref)))
    ]
    key_copy = pltpu.make_async_copy(kc_hbm, kc_ref, sems.at[4])
    value_copy = pltpu.make_async_copy(vc_hbm, vc_ref, sems.at[5])
    wo_copy = pltpu.make_async_copy(wo_hbm, wo_ref, sems.at[6])
    for copy in (*small, key_copy, value_copy, wo_copy):
        copy.start()

    for copy in small:
        copy.wait()
    r = lax.broadcasted_iota(jnp.int32, (rows, rows), 0)
    c = lax.broadcasted_iota(jnp.int32, (rows, rows), 1)
    lengths = jnp.sum(jnp.where(r == c, len_ref[...], 0).astype(F32), axis=1, keepdims=True)
    span = group * positions
    row_token = lax.broadcasted_iota(jnp.int32, (heads * group, span), 0) % group
    column = lax.broadcasted_iota(jnp.int32, (heads * group, span), 1)
    own_column = column - row_token * positions
    own_position = jnp.where(own_column >= 0, own_column, positions).astype(F32)

    def per_head(rows_of_group):
        return jnp.concatenate([rows_of_group] * heads, axis=0)

    def group_rows(ref, g):
        pair = ref[pl.ds(g // 2 * 2 * group, 2 * group), :].astype(F32)
        return pair[g % 2 * group : (g % 2 + 1) * group]

    groups = rows // group
    scores, own_scores, raised, own_raised, outs = [], [], [], [], []
    key_copy.wait()
    for g in range(groups):
        q_rows = group_rows(q_ref, g)
        q = jnp.concatenate([q_rows[:, h * LANES : (h + 1) * LANES] for h in range(heads)], axis=0)
        keys = kc_ref[pl.ds(g * span, span), :]
        score = lax.dot_general(q.astype(BF16), keys, (((1,), (1,)), ((), ())), preferred_element_type=F32)
        scores.append(jnp.where(own_position < per_head(lengths[g * group : (g + 1) * group]), score, -jnp.inf))
        own_scores.append(jnp.sum(q * per_head(group_rows(nk_ref, g)), axis=1, keepdims=True))
    for score, own_score in zip(scores, own_scores):
        highest = jnp.maximum(jnp.max(score, axis=1, keepdims=True), own_score)
        raised.append(jnp.exp2((score - highest) * to_exponent))
        own_raised.append(jnp.exp2((own_score - highest) * to_exponent))
    value_copy.wait()
    for g in range(groups):
        inverse = 1.0 / (jnp.sum(raised[g], axis=1, keepdims=True) + own_raised[g])
        values = vc_ref[pl.ds(g * span, span), :]
        out = jnp.dot(raised[g].astype(BF16), values, preferred_element_type=F32)
        outs.append((out + own_raised[g] * per_head(group_rows(nv_ref, g))) * inverse)
    for g in range(0, groups, 2):
        place = lax.rem(g * group + half * (1 - sec_ref[0]), rows)
        place = pl.multiple_of(place, 2 * group)
        for h in range(heads):
            pair = [outs[g + j][h * group : (h + 1) * group] for j in range(2)]
            attn_ref[pl.ds(place, 2 * group), pl.ds(h * LANES, LANES)] = jnp.concatenate(pair, axis=0).astype(BF16)

    wo_copy.wait()
    proj = jnp.dot(attn_ref[...], wo_ref[...], preferred_element_type=F32)
    theirs_ref[...] = proj[:half].astype(BF16)
    mine_ref[...] = proj[half:].astype(BF16)


def attend(sec, lengths, q, kc, vc, nk, nv, wo):
    rows, head_width = q.shape
    width = wo.shape[1]
    out = jax.ShapeDtypeStruct((rows // 2, width), BF16)
    far = [pltpu.with_memory_space_constraint(a, pltpu.HBM) for a in (lengths, q, kc, vc, nk, nv, wo)]
    return pl.pallas_call(
        attend_kernel,
        in_specs=[whole(SMEM)] + [whole(pltpu.HBM)] * 7,
        out_specs=[whole(), whole()],
        out_shape=[out, out],
        scratch_shapes=[pltpu.VMEM(a.shape, a.dtype) for a in (lengths, q, kc, vc, nk, nv)]
        + [
            pltpu.VMEM(wo.shape, BF16),
            pltpu.VMEM((rows, head_width), BF16),
            pltpu.SemaphoreType.DMA((7,)),
        ],
        compiler_params=pltpu.CompilerParams(vmem_limit_bytes=14 * MIB),
        name="attend",
    )(sec, *far)


def quarter_kernel(kv_ref, mine_ref, got_ref, *out_refs):
    count = len(out_refs)
    rows = mine_ref.shape[0] // count
    for step, out_ref in enumerate(out_refs):
        at = pl.ds(pl.multiple_of(lax.rem(kv_ref[0] + step, count) * rows, rows), rows)
        out_ref[...] = (mine_ref[at, :].astype(F32) + got_ref[at, :].astype(F32)).astype(BF16)


def quarter(kv, mine, got, count):
    rows, width = mine.shape
    out = jax.ShapeDtypeStruct((rows // count, width), BF16)
    return pl.pallas_call(
        quarter_kernel,
        in_specs=[whole(SMEM), whole(), whole()],
        out_specs=[whole()] * count,
        out_shape=[out] * count,
        compiler_params=pltpu.CompilerParams(vmem_limit_bytes=4 * MIB),
        name="quarter",
    )(kv, mine, got)


def route_kernel(ids_ref, slots_ref, *refs):
    part_refs, (residual_ref, gain_ref, stream_hbm, out_ref, wide_ref, stream_ref, sem) = refs[:-7], refs[-7:]
    rows, width = residual_ref.shape
    pieces = width // LANES
    top = ids_ref.shape[0]
    stride = pieces + GAP
    out_ref[...] = jnp.zeros_like(out_ref)
    proj = part_refs[0][...].astype(F32)
    for part_ref in part_refs[1:]:
        proj = proj + part_ref[...].astype(F32)
    stream = (residual_ref[...].astype(F32) + proj).astype(BF16)
    stream_ref[...] = stream
    leave = pltpu.make_async_copy(stream_ref, stream_hbm, sem)
    leave.start()
    widened = stream.astype(F32)
    mean_square = jnp.mean(widened * widened, axis=-1, keepdims=True)
    normed = widened * lax.rsqrt(mean_square + 1e-06) * gain_ref[...]
    for t in range(0, rows, 8):
        for s in range(pieces):
            wide_ref[pl.ds(t * stride + s, 8, stride=stride), :] = normed[t : t + 8, s * LANES : (s + 1) * LANES]

    def one(t, carry):
        row = wide_ref[pl.ds(t * stride, pieces), :].astype(BF16)
        for k in range(top):
            out_ref[ids_ref[k, t], slots_ref[k, t]] = row
        return carry

    lax.fori_loop(0, rows, one, 0, unroll=4)
    leave.wait()


def route(ids, slots, parts, residual, gain, expert_count, capacity):
    rows, width = residual.shape
    pieces = width // LANES
    return pl.pallas_call(
        route_kernel,
        in_specs=[whole(SMEM), whole(SMEM)] + [whole()] * (len(parts) + 2),
        out_specs=[whole(pl.ANY), whole()],
        out_shape=[
            jax.ShapeDtypeStruct((rows, width), BF16),
            jax.ShapeDtypeStruct((expert_count, capacity, pieces, LANES), BF16),
        ],
        scratch_shapes=[
            pltpu.VMEM((rows * (pieces + GAP), LANES), F32),
            pltpu.VMEM((rows, width), BF16),
            pltpu.SemaphoreType.DMA,
        ],
        compiler_params=pltpu.CompilerParams(vmem_limit_bytes=4 * MIB),
        name="route",
    )(ids, slots, *parts, residual, gain)


def load_kernel(*refs):
    count = len(refs) // 2
    sems = refs[-1]
    copies = [pltpu.make_async_copy(refs[i], refs[count + i], sems.at[i]) for i in range(count)]
    for copy in copies:
        copy.start()
    for copy in copies:
        copy.wait()


def load(*weights):
    size = sum(w.size * 2 for w in weights)
    return pl.pallas_call(
        load_kernel,
        in_specs=[whole(pltpu.HBM)] * len(weights),
        out_specs=[whole()] * len(weights),
        out_shape=[pltpu.VMEM(w.shape, w.dtype) for w in weights],
        scratch_shapes=[pltpu.SemaphoreType.DMA((len(weights),))],
        compiler_params=pltpu.CompilerParams(vmem_limit_bytes=2 * MIB),
        cost_estimate=pl.CostEstimate(flops=0, bytes_accessed=2 * size, transcendentals=0),
        name="load",
    )(*[pltpu.with_memory_space_constraint(w, pltpu.HBM) for w in weights])


def expert_kernel(x_ref, wg_ref, wu_ref, wd_hbm, out_ref, wide_ref, flat_ref, hidden_ref, wd_ref, sem):
    rows, pieces, _ = x_ref.shape
    hidden_width = wg_ref.shape[1]
    width = pieces * LANES
    stride = pieces + GAP
    ncols = 256
    dcols = 1024
    group = 16
    down_copy = pltpu.make_async_copy(wd_hbm, wd_ref, sem)
    down_copy.start()

    def spread(i, carry):
        base = pl.multiple_of(i * group, group)
        for r in range(group):
            wide_ref[pl.ds(r * stride, pieces), :] = x_ref[base + r].astype(F32)
        for s in range(pieces):
            low = wide_ref[pl.ds(s, 8, stride=stride), :]
            high = wide_ref[pl.ds(8 * stride + s, 8, stride=stride), :]
            flat_ref[pl.ds(base, group), pl.ds(s * LANES, LANES)] = jnp.concatenate([low, high], axis=0).astype(BF16)
        return carry

    lax.fori_loop(0, rows // group, spread, 0)

    for n in range(hidden_width // ncols):
        at = pl.ds(n * ncols, ncols)
        gate = jnp.dot(flat_ref[...], wg_ref[:, at], preferred_element_type=F32)
        up = jnp.dot(flat_ref[...], wu_ref[:, at], preferred_element_type=F32)
        hidden_ref[:, at] = (gate / (1.0 + jnp.exp(-gate)) * up).astype(BF16)

    down_copy.wait()
    for n in range(width // dcols):
        done = jnp.dot(hidden_ref[...], wd_ref[:, pl.ds(n * dcols, dcols)], preferred_element_type=F32)
        for r in range(0, rows, 8):
            for s in range(dcols // LANES):
                wide_ref[pl.ds(r * stride + n * (dcols // LANES) + s, 8, stride=stride), :] = done[
                    r : r + 8, s * LANES : (s + 1) * LANES
                ]

    def narrow(i, carry):
        base = pl.multiple_of(i * group, group)
        for r in range(group):
            out_ref[base + r] = wide_ref[pl.ds((base + r) * stride, pieces), :].astype(BF16)
        return carry

    lax.fori_loop(0, rows // group, narrow, 0)


def expert(x, wg, wu, wd):
    rows, pieces, _ = x.shape
    width, hidden_width = wg.shape
    near = [pltpu.with_memory_space_constraint(w, pltpu.VMEM) for w in (wg, wu)]
    return pl.pallas_call(
        expert_kernel,
        in_specs=[whole()] * 3 + [whole(pltpu.HBM)],
        out_specs=whole(),
        out_shape=jax.ShapeDtypeStruct(x.shape, BF16),
        scratch_shapes=[
            pltpu.VMEM((rows * (pieces + GAP), LANES), F32),
            pltpu.VMEM((rows, width), BF16),
            pltpu.VMEM((rows, hidden_width), BF16),
            pltpu.VMEM(wd.shape, BF16),
            pltpu.SemaphoreType.DMA,
        ],
        compiler_params=pltpu.CompilerParams(vmem_limit_bytes=20 * MIB),
        name="expert",
    )(x, *near, pltpu.with_memory_space_constraint(wd, pltpu.HBM))


def combine_kernel(ids_ref, slots_ref, probs_ref, rows_ref, out_ref, wide_ref):
    rows, width = out_ref.shape
    pieces = width // LANES
    top = ids_ref.shape[0]
    stride = pieces + GAP

    def one(t, carry):
        total = None
        for k in range(top):
            term = rows_ref[ids_ref[k, t], slots_ref[k, t]].astype(F32) * probs_ref[k, t]
            total = term if total is None else total + term
        wide_ref[pl.ds(t * stride, pieces), :] = total
        return carry

    lax.fori_loop(0, rows, one, 0, unroll=4)
    for s in range(pieces):
        low = wide_ref[pl.ds(s, 8, stride=stride), :]
        high = wide_ref[pl.ds(8 * stride + s, 8, stride=stride), :]
        out_ref[:, pl.ds(s * LANES, LANES)] = jnp.concatenate([low, high], axis=0).astype(BF16)


def combine(ids, slots, probs, returned, width):
    rows = ids.shape[1]
    return pl.pallas_call(
        combine_kernel,
        in_specs=[whole(SMEM)] * 3 + [whole()],
        out_specs=whole(),
        out_shape=jax.ShapeDtypeStruct((rows, width), BF16),
        scratch_shapes=[pltpu.VMEM((rows * (width // LANES + GAP), LANES), F32)],
        compiler_params=pltpu.CompilerParams(vmem_limit_bytes=4 * MIB),
        name="combine",
    )(ids, slots, probs, returned)


def on_device(
    queries,
    key_cache,
    value_cache,
    new_keys,
    new_values,
    lengths,
    out_proj,
    residual,
    norm_gain,
    expert_ids,
    expert_slots,
    gate_probs,
    w_gate,
    w_up,
    w_down,
):
    row_count = queries.shape[0]
    width = out_proj.shape[1]
    pieces = width // LANES
    sec_count, group_count = lax.axis_size("sec"), lax.axis_size("kv")
    expert_count = sec_count * lax.axis_size("req") * group_count
    row_share, top_count = expert_ids.shape
    capacity = top_count * row_share // expert_count + 1
    sec = lax.axis_index("sec").astype(jnp.int32).reshape(1)
    kv = lax.axis_index("kv").astype(jnp.int32).reshape(1)

    theirs, mine = attend(
        sec,
        lengths.reshape(1, row_count),
        queries,
        key_cache.reshape(-1, LANES),
        value_cache.reshape(-1, LANES),
        new_keys.reshape(row_count, LANES),
        new_values.reshape(row_count, LANES),
        out_proj,
    )
    got = lax.ppermute(theirs, "sec", [(i, 1 - i) for i in range(sec_count)])
    quarters = quarter(kv, mine, got, group_count)
    parts = [quarters[0]] + [
        lax.ppermute(quarters[s], "kv", [(i, (i + s) % group_count) for i in range(group_count)])
        for s in range(1, group_count)
    ]
    ids, slots, probs = expert_ids.T, expert_slots.T, gate_probs.T
    stream, outgoing = route(ids, slots, parts, residual, norm_gain.reshape(1, width), expert_count, capacity)

    def exchange(rows):
        sent = rows.reshape(expert_count, capacity * pieces, LANES)
        return lax.all_to_all(sent, ("sec", "req", "kv"), split_axis=0, concat_axis=0, tiled=True)

    outgoing, *weights = lax.optimization_barrier((outgoing, *load(w_gate[0], w_up[0])))
    arrived = exchange(outgoing).reshape(expert_count * capacity, pieces, LANES)
    finished = expert(arrived, *weights, w_down[0])
    returned = exchange(finished).reshape(expert_count, capacity, pieces, LANES)
    moe_out = combine(ids, slots, probs, returned, width)
    return (stream, moe_out)


def solution(mesh):
    return jax.shard_map(
        on_device,
        mesh=mesh,
        in_specs=(
            P("req", ("kv", "sec")),
            P("req", "kv", None, None),
            P("req", "kv", None, None),
            P("req", "kv", None),
            P("req", "kv", None),
            P("req"),
            P(("kv", "sec"), None),
            P(("req", "sec", "kv"), None),
            P(),
            P(("req", "sec", "kv"), None),
            P(("req", "sec", "kv"), None),
            P(("req", "sec", "kv"), None),
            P(("sec", "req", "kv"), None, None),
            P(("sec", "req", "kv"), None, None),
            P(("sec", "req", "kv"), None, None),
        ),
        out_specs=(P(("req", "sec", "kv"), None), P(("req", "sec", "kv"), None)),
        check_vma=False,
    )
```

```python
import math

import jax
import jax.numpy as jnp
from jax import lax
from jax.experimental import pallas as pl
from jax.experimental.pallas import tpu as pltpu
from jax.sharding import PartitionSpec as P

LANES = 128
F32 = jnp.float32
BF16 = jnp.bfloat16
MIB = 1 << 20

GAP = 1

VMEM = pltpu.VMEM
SMEM = pltpu.SMEM


def whole(space=VMEM):
    return pl.BlockSpec(memory_space=space)


def attend_kernel(
    sec_ref,
    len_hbm,
    q_hbm,
    kc_hbm,
    vc_hbm,
    nk_hbm,
    nv_hbm,
    wo_hbm,
    theirs_ref,
    mine_ref,
    len_ref,
    q_ref,
    kc_ref,
    vc_ref,
    nk_ref,
    nv_ref,
    wo_ref,
    attn_ref,
    sems,
):
    rows, head_width = q_ref.shape
    heads = head_width // LANES
    positions = kc_ref.shape[0] // rows
    group = 8
    to_exponent = math.log2(math.e) / LANES**0.5
    half = rows // 2

    small = [
        pltpu.make_async_copy(source, target, sems.at[i])
        for i, (source, target) in enumerate(((len_hbm, len_ref), (q_hbm, q_ref), (nk_hbm, nk_ref), (nv_hbm, nv_ref)))
    ]
    key_copy = pltpu.make_async_copy(kc_hbm, kc_ref, sems.at[4])
    value_copy = pltpu.make_async_copy(vc_hbm, vc_ref, sems.at[5])
    wo_copy = pltpu.make_async_copy(wo_hbm, wo_ref, sems.at[6])
    for copy in (*small, key_copy, value_copy, wo_copy):
        copy.start()

    for copy in small:
        copy.wait()
    r = lax.broadcasted_iota(jnp.int32, (rows, rows), 0)
    c = lax.broadcasted_iota(jnp.int32, (rows, rows), 1)
    lengths = jnp.sum(jnp.where(r == c, len_ref[...], 0).astype(F32), axis=1, keepdims=True)
    span = group * positions
    row_token = lax.broadcasted_iota(jnp.int32, (heads * group, span), 0) % group
    column = lax.broadcasted_iota(jnp.int32, (heads * group, span), 1)
    own_column = column - row_token * positions
    own_position = jnp.where(own_column >= 0, own_column, positions).astype(F32)

    def per_head(rows_of_group):
        return jnp.concatenate([rows_of_group] * heads, axis=0)

    def group_rows(ref, g):
        pair = ref[pl.ds(g // 2 * 2 * group, 2 * group), :].astype(F32)
        return pair[g % 2 * group : (g % 2 + 1) * group]

    groups = rows // group
    scores, own_scores, raised, own_raised, outs = [], [], [], [], []
    key_copy.wait()
    for g in range(groups):
        q_rows = group_rows(q_ref, g)
        q = jnp.concatenate([q_rows[:, h * LANES : (h + 1) * LANES] for h in range(heads)], axis=0)
        keys = kc_ref[pl.ds(g * span, span), :]
        score = lax.dot_general(q.astype(BF16), keys, (((1,), (1,)), ((), ())), preferred_element_type=F32)
        scores.append(jnp.where(own_position < per_head(lengths[g * group : (g + 1) * group]), score, -jnp.inf))
        own_scores.append(jnp.sum(q * per_head(group_rows(nk_ref, g)), axis=1, keepdims=True))
    for score, own_score in zip(scores, own_scores):
        highest = jnp.maximum(jnp.max(score, axis=1, keepdims=True), own_score)
        raised.append(jnp.exp2((score - highest) * to_exponent))
        own_raised.append(jnp.exp2((own_score - highest) * to_exponent))
    value_copy.wait()
    for g in range(groups):
        inverse = 1.0 / (jnp.sum(raised[g], axis=1, keepdims=True) + own_raised[g])
        values = vc_ref[pl.ds(g * span, span), :]
        out = jnp.dot(raised[g].astype(BF16), values, preferred_element_type=F32)
        outs.append((out + own_raised[g] * per_head(group_rows(nv_ref, g))) * inverse)
    for g in range(0, groups, 2):
        place = lax.rem(g * group + half * (1 - sec_ref[0]), rows)
        place = pl.multiple_of(place, 2 * group)
        for h in range(heads):
            pair = [outs[g + j][h * group : (h + 1) * group] for j in range(2)]
            attn_ref[pl.ds(place, 2 * group), pl.ds(h * LANES, LANES)] = jnp.concatenate(pair, axis=0).astype(BF16)

    wo_copy.wait()
    proj = jnp.dot(attn_ref[...], wo_ref[...], preferred_element_type=F32)
    theirs_ref[...] = proj[:half].astype(BF16)
    mine_ref[...] = proj[half:].astype(BF16)


def attend(sec, lengths, q, kc, vc, nk, nv, wo):
    rows, head_width = q.shape
    width = wo.shape[1]
    out = jax.ShapeDtypeStruct((rows // 2, width), BF16)
    far = [pltpu.with_memory_space_constraint(a, pltpu.HBM) for a in (lengths, q, kc, vc, nk, nv, wo)]
    return pl.pallas_call(
        attend_kernel,
        in_specs=[whole(SMEM)] + [whole(pltpu.HBM)] * 7,
        out_specs=[whole(), whole()],
        out_shape=[out, out],
        scratch_shapes=[pltpu.VMEM(a.shape, a.dtype) for a in (lengths, q, kc, vc, nk, nv)]
        + [
            pltpu.VMEM(wo.shape, BF16),
            pltpu.VMEM((rows, head_width), BF16),
            pltpu.SemaphoreType.DMA((7,)),
        ],
        compiler_params=pltpu.CompilerParams(vmem_limit_bytes=14 * MIB),
        name="attend",
    )(sec, *far)


def quarter_kernel(kv_ref, mine_ref, got_ref, *out_refs):
    count = len(out_refs)
    rows = mine_ref.shape[0] // count
    for step, out_ref in enumerate(out_refs):
        at = pl.ds(pl.multiple_of(lax.rem(kv_ref[0] + step, count) * rows, rows), rows)
        out_ref[...] = (mine_ref[at, :].astype(F32) + got_ref[at, :].astype(F32)).astype(BF16)


def quarter(kv, mine, got, count):
    rows, width = mine.shape
    out = jax.ShapeDtypeStruct((rows // count, width), BF16)
    return pl.pallas_call(
        quarter_kernel,
        in_specs=[whole(SMEM), whole(), whole()],
        out_specs=[whole()] * count,
        out_shape=[out] * count,
        compiler_params=pltpu.CompilerParams(vmem_limit_bytes=4 * MIB),
        name="quarter",
    )(kv, mine, got)


def route_kernel(ids_ref, slots_ref, *refs):
    part_refs, (residual_ref, gain_ref, stream_hbm, out_ref, wide_ref, stream_ref, sem) = refs[:-7], refs[-7:]
    rows, width = residual_ref.shape
    pieces = width // LANES
    top = ids_ref.shape[0]
    stride = pieces + GAP
    out_ref[...] = jnp.zeros_like(out_ref)
    proj = part_refs[0][...].astype(F32)
    for part_ref in part_refs[1:]:
        proj = proj + part_ref[...].astype(F32)
    stream = (residual_ref[...].astype(F32) + proj).astype(BF16)
    stream_ref[...] = stream
    leave = pltpu.make_async_copy(stream_ref, stream_hbm, sem)
    leave.start()
    widened = stream.astype(F32)
    mean_square = jnp.mean(widened * widened, axis=-1, keepdims=True)
    normed = widened * lax.rsqrt(mean_square + 1e-06) * gain_ref[...]
    for t in range(0, rows, 8):
        for s in range(pieces):
            wide_ref[pl.ds(t * stride + s, 8, stride=stride), :] = normed[t : t + 8, s * LANES : (s + 1) * LANES]

    def one(t, carry):
        row = wide_ref[pl.ds(t * stride, pieces), :].astype(BF16)
        for k in range(top):
            out_ref[ids_ref[k, t], slots_ref[k, t]] = row
        return carry

    lax.fori_loop(0, rows, one, 0, unroll=4)
    leave.wait()


def route(ids, slots, parts, residual, gain, expert_count, capacity):
    rows, width = residual.shape
    pieces = width // LANES
    return pl.pallas_call(
        route_kernel,
        in_specs=[whole(SMEM), whole(SMEM)] + [whole()] * (len(parts) + 2),
        out_specs=[whole(pl.ANY), whole()],
        out_shape=[
            jax.ShapeDtypeStruct((rows, width), BF16),
            jax.ShapeDtypeStruct((expert_count, capacity, pieces, LANES), BF16),
        ],
        scratch_shapes=[
            pltpu.VMEM((rows * (pieces + GAP), LANES), F32),
            pltpu.VMEM((rows, width), BF16),
            pltpu.SemaphoreType.DMA,
        ],
        compiler_params=pltpu.CompilerParams(vmem_limit_bytes=4 * MIB),
        name="route",
    )(ids, slots, *parts, residual, gain)


def load_kernel(*refs):
    count = len(refs) // 2
    sems = refs[-1]
    copies = [pltpu.make_async_copy(refs[i], refs[count + i], sems.at[i]) for i in range(count)]
    for copy in copies:
        copy.start()
    for copy in copies:
        copy.wait()


def load(weights, tables):
    size = sum(w.size * 2 for w in weights)
    arrays = [*weights, *tables]
    out = pl.pallas_call(
        load_kernel,
        in_specs=[whole(pltpu.HBM)] * len(arrays),
        out_specs=[whole()] * len(weights) + [whole(SMEM)] * len(tables),
        out_shape=[pltpu.VMEM(w.shape, w.dtype) for w in weights] + [pltpu.SMEM(t.shape, t.dtype) for t in tables],
        scratch_shapes=[pltpu.SemaphoreType.DMA((len(arrays),))],
        compiler_params=pltpu.CompilerParams(vmem_limit_bytes=2 * MIB),
        cost_estimate=pl.CostEstimate(flops=0, bytes_accessed=2 * size, transcendentals=0),
        name="load",
    )(*[pltpu.with_memory_space_constraint(a, pltpu.HBM) for a in arrays])
    return out[: len(weights)], out[len(weights) :]


def expert_kernel(x_ref, wg_ref, wu_ref, wd_hbm, out_ref, wide_ref, flat_ref, hidden_ref, wd_ref, sem):
    rows, pieces, _ = x_ref.shape
    hidden_width = wg_ref.shape[1]
    width = pieces * LANES
    stride = pieces + GAP
    ncols = 256
    dcols = 1024
    group = 16
    down_copy = pltpu.make_async_copy(wd_hbm, wd_ref, sem)
    down_copy.start()

    def spread(i, carry):
        base = pl.multiple_of(i * group, group)
        for r in range(group):
            wide_ref[pl.ds(r * stride, pieces), :] = x_ref[base + r].astype(F32)
        for s in range(pieces):
            low = wide_ref[pl.ds(s, 8, stride=stride), :]
            high = wide_ref[pl.ds(8 * stride + s, 8, stride=stride), :]
            flat_ref[pl.ds(base, group), pl.ds(s * LANES, LANES)] = jnp.concatenate([low, high], axis=0).astype(BF16)
        return carry

    lax.fori_loop(0, rows // group, spread, 0)

    for n in range(hidden_width // ncols):
        at = pl.ds(n * ncols, ncols)
        gate = jnp.dot(flat_ref[...], wg_ref[:, at], preferred_element_type=F32)
        up = jnp.dot(flat_ref[...], wu_ref[:, at], preferred_element_type=F32)
        hidden_ref[:, at] = (gate / (1.0 + jnp.exp(-gate)) * up).astype(BF16)

    down_copy.wait()
    for n in range(width // dcols):
        done = jnp.dot(hidden_ref[...], wd_ref[:, pl.ds(n * dcols, dcols)], preferred_element_type=F32)
        for r in range(0, rows, 8):
            for s in range(dcols // LANES):
                wide_ref[pl.ds(r * stride + n * (dcols // LANES) + s, 8, stride=stride), :] = done[
                    r : r + 8, s * LANES : (s + 1) * LANES
                ]

    def narrow(i, carry):
        base = pl.multiple_of(i * group, group)
        for r in range(group):
            out_ref[base + r] = wide_ref[pl.ds((base + r) * stride, pieces), :].astype(BF16)
        return carry

    lax.fori_loop(0, rows // group, narrow, 0)


def expert(x, wg, wu, wd):
    rows, pieces, _ = x.shape
    width, hidden_width = wg.shape
    near = [pltpu.with_memory_space_constraint(w, pltpu.VMEM) for w in (wg, wu)]
    return pl.pallas_call(
        expert_kernel,
        in_specs=[whole()] * 3 + [whole(pltpu.HBM)],
        out_specs=whole(),
        out_shape=jax.ShapeDtypeStruct(x.shape, BF16),
        scratch_shapes=[
            pltpu.VMEM((rows * (pieces + GAP), LANES), F32),
            pltpu.VMEM((rows, width), BF16),
            pltpu.VMEM((rows, hidden_width), BF16),
            pltpu.VMEM(wd.shape, BF16),
            pltpu.SemaphoreType.DMA,
        ],
        compiler_params=pltpu.CompilerParams(vmem_limit_bytes=20 * MIB),
        name="expert",
    )(x, *near, pltpu.with_memory_space_constraint(wd, pltpu.HBM))


def combine_kernel(ids_ref, slots_ref, probs_ref, rows_ref, out_ref, wide_ref):
    rows, width = out_ref.shape
    pieces = width // LANES
    top = ids_ref.shape[0]
    stride = pieces + GAP

    def one(t, carry):
        total = None
        for k in range(top):
            term = rows_ref[ids_ref[k, t], slots_ref[k, t]].astype(F32) * probs_ref[k, t]
            total = term if total is None else total + term
        wide_ref[pl.ds(t * stride, pieces), :] = total
        return carry

    lax.fori_loop(0, rows, one, 0, unroll=4)
    for s in range(pieces):
        low = wide_ref[pl.ds(s, 8, stride=stride), :]
        high = wide_ref[pl.ds(8 * stride + s, 8, stride=stride), :]
        out_ref[:, pl.ds(s * LANES, LANES)] = jnp.concatenate([low, high], axis=0).astype(BF16)


def combine(ids, slots, probs, returned, width):
    rows = ids.shape[1]
    return pl.pallas_call(
        combine_kernel,
        in_specs=[whole(SMEM)] * 3 + [whole()],
        out_specs=whole(),
        out_shape=jax.ShapeDtypeStruct((rows, width), BF16),
        scratch_shapes=[pltpu.VMEM((rows * (width // LANES + GAP), LANES), F32)],
        compiler_params=pltpu.CompilerParams(vmem_limit_bytes=4 * MIB),
        name="combine",
    )(ids, slots, probs, returned)


def on_device(
    queries,
    key_cache,
    value_cache,
    new_keys,
    new_values,
    lengths,
    out_proj,
    residual,
    norm_gain,
    expert_ids,
    expert_slots,
    gate_probs,
    w_gate,
    w_up,
    w_down,
):
    row_count = queries.shape[0]
    width = out_proj.shape[1]
    pieces = width // LANES
    sec_count, group_count = lax.axis_size("sec"), lax.axis_size("kv")
    expert_count = sec_count * lax.axis_size("req") * group_count
    row_share, top_count = expert_ids.shape
    capacity = top_count * row_share // expert_count + 1
    sec = lax.axis_index("sec").astype(jnp.int32).reshape(1)
    kv = lax.axis_index("kv").astype(jnp.int32).reshape(1)

    theirs, mine = attend(
        sec,
        lengths.reshape(1, row_count),
        queries,
        key_cache.reshape(-1, LANES),
        value_cache.reshape(-1, LANES),
        new_keys.reshape(row_count, LANES),
        new_values.reshape(row_count, LANES),
        out_proj,
    )
    got = lax.ppermute(theirs, "sec", [(i, 1 - i) for i in range(sec_count)])
    quarters = quarter(kv, mine, got, group_count)
    parts = [quarters[0]]
    for s in sorted(range(1, group_count), key=lambda s: min(s, group_count - s)):
        parts.append(lax.ppermute(quarters[s], "kv", [(i, (i + s) % group_count) for i in range(group_count)]))
    weights, tables = load((w_gate[0], w_up[0]), (expert_ids.T, expert_slots.T, gate_probs.T))
    ids, slots, probs = tables
    stream, outgoing = route(ids, slots, parts, residual, norm_gain.reshape(1, width), expert_count, capacity)

    def exchange(rows):
        sent = rows.reshape(expert_count, capacity * pieces, LANES)
        return lax.all_to_all(sent, ("sec", "req", "kv"), split_axis=0, concat_axis=0, tiled=True)

    outgoing, *weights = lax.optimization_barrier((outgoing, *weights))
    arrived = exchange(outgoing).reshape(expert_count * capacity, pieces, LANES)
    finished = expert(arrived, *weights, w_down[0])
    returned = exchange(finished).reshape(expert_count, capacity, pieces, LANES)
    moe_out = combine(ids, slots, probs, returned, width)
    return (stream, moe_out)


def solution(mesh):
    return jax.shard_map(
        on_device,
        mesh=mesh,
        in_specs=(
            P("req", ("kv", "sec")),
            P("req", "kv", None, None),
            P("req", "kv", None, None),
            P("req", "kv", None),
            P("req", "kv", None),
            P("req"),
            P(("kv", "sec"), None),
            P(("req", "sec", "kv"), None),
            P(),
            P(("req", "sec", "kv"), None),
            P(("req", "sec", "kv"), None),
            P(("req", "sec", "kv"), None),
            P(("sec", "req", "kv"), None, None),
            P(("sec", "req", "kv"), None, None),
            P(("sec", "req", "kv"), None, None),
        ),
        out_specs=(P(("req", "sec", "kv"), None), P(("req", "sec", "kv"), None)),
        check_vma=False,
    )
```

```python
import math

import jax
import jax.numpy as jnp
from jax import lax
from jax.experimental import pallas as pl
from jax.experimental.pallas import tpu as pltpu
from jax.sharding import PartitionSpec as P

LANES = 128
F32 = jnp.float32
BF16 = jnp.bfloat16
MIB = 1 << 20

GAP = 1
SPARE = 40

VMEM = pltpu.VMEM
SMEM = pltpu.SMEM


def whole(space=VMEM):
    return pl.BlockSpec(memory_space=space)


def attend_kernel(
    sec_ref,
    len_hbm,
    q_hbm,
    kc_hbm,
    vc_hbm,
    nk_hbm,
    nv_hbm,
    wo_hbm,
    theirs_ref,
    mine_ref,
    len_ref,
    q_ref,
    kc_ref,
    vc_ref,
    nk_ref,
    nv_ref,
    wo_ref,
    attn_ref,
    sems,
):
    rows, head_width = q_ref.shape
    heads = head_width // LANES
    positions = kc_ref.shape[0] // rows
    group = 8
    to_exponent = math.log2(math.e) / LANES**0.5
    half = rows // 2

    small = [
        pltpu.make_async_copy(source, target, sems.at[i])
        for i, (source, target) in enumerate(((len_hbm, len_ref), (q_hbm, q_ref), (nk_hbm, nk_ref), (nv_hbm, nv_ref)))
    ]
    key_copy = pltpu.make_async_copy(kc_hbm, kc_ref, sems.at[4])
    value_copy = pltpu.make_async_copy(vc_hbm, vc_ref, sems.at[5])
    wo_copy = pltpu.make_async_copy(wo_hbm, wo_ref, sems.at[6])
    for copy in (*small, key_copy, value_copy, wo_copy):
        copy.start()

    for copy in small:
        copy.wait()
    r = lax.broadcasted_iota(jnp.int32, (rows, rows), 0)
    c = lax.broadcasted_iota(jnp.int32, (rows, rows), 1)
    lengths = jnp.sum(jnp.where(r == c, len_ref[...], 0).astype(F32), axis=1, keepdims=True)
    span = group * positions
    row_token = lax.broadcasted_iota(jnp.int32, (heads * group, span), 0) % group
    column = lax.broadcasted_iota(jnp.int32, (heads * group, span), 1)
    own_column = column - row_token * positions
    own_position = jnp.where(own_column >= 0, own_column, positions).astype(F32)

    def per_head(rows_of_group):
        return jnp.concatenate([rows_of_group] * heads, axis=0)

    def group_rows(ref, g):
        pair = ref[pl.ds(g // 2 * 2 * group, 2 * group), :].astype(F32)
        return pair[g % 2 * group : (g % 2 + 1) * group]

    groups = rows // group
    scores, own_scores, raised, own_raised, outs = [], [], [], [], []
    key_copy.wait()
    for g in range(groups):
        q_rows = group_rows(q_ref, g)
        q = jnp.concatenate([q_rows[:, h * LANES : (h + 1) * LANES] for h in range(heads)], axis=0)
        keys = kc_ref[pl.ds(g * span, span), :]
        score = lax.dot_general(q.astype(BF16), keys, (((1,), (1,)), ((), ())), preferred_element_type=F32)
        scores.append(jnp.where(own_position < per_head(lengths[g * group : (g + 1) * group]), score, -jnp.inf))
        own_scores.append(jnp.sum(q * per_head(group_rows(nk_ref, g)), axis=1, keepdims=True))
    for score, own_score in zip(scores, own_scores):
        highest = jnp.maximum(jnp.max(score, axis=1, keepdims=True), own_score)
        raised.append(jnp.exp2((score - highest) * to_exponent))
        own_raised.append(jnp.exp2((own_score - highest) * to_exponent))
    value_copy.wait()
    for g in range(groups):
        inverse = 1.0 / (jnp.sum(raised[g], axis=1, keepdims=True) + own_raised[g])
        values = vc_ref[pl.ds(g * span, span), :]
        out = jnp.dot(raised[g].astype(BF16), values, preferred_element_type=F32)
        outs.append((out + own_raised[g] * per_head(group_rows(nv_ref, g))) * inverse)
    for g in range(0, groups, 2):
        place = lax.rem(g * group + half * (1 - sec_ref[0]), rows)
        place = pl.multiple_of(place, 2 * group)
        for h in range(heads):
            pair = [outs[g + j][h * group : (h + 1) * group] for j in range(2)]
            attn_ref[pl.ds(place, 2 * group), pl.ds(h * LANES, LANES)] = jnp.concatenate(pair, axis=0).astype(BF16)

    wo_copy.wait()
    proj = jnp.dot(attn_ref[...], wo_ref[...], preferred_element_type=F32)
    theirs_ref[...] = proj[:half].astype(BF16)
    mine_ref[...] = proj[half:].astype(BF16)


def attend(sec, lengths, q, kc, vc, nk, nv, wo):
    rows, head_width = q.shape
    width = wo.shape[1]
    out = jax.ShapeDtypeStruct((rows // 2, width), BF16)
    far = [pltpu.with_memory_space_constraint(a, pltpu.HBM) for a in (lengths, q, kc, vc, nk, nv, wo)]
    return pl.pallas_call(
        attend_kernel,
        in_specs=[whole(SMEM)] + [whole(pltpu.HBM)] * 7,
        out_specs=[whole(), whole()],
        out_shape=[out, out],
        scratch_shapes=[pltpu.VMEM(a.shape, a.dtype) for a in (lengths, q, kc, vc, nk, nv)]
        + [
            pltpu.VMEM(wo.shape, BF16),
            pltpu.VMEM((rows, head_width), BF16),
            pltpu.SemaphoreType.DMA((7,)),
        ],
        compiler_params=pltpu.CompilerParams(vmem_limit_bytes=14 * MIB),
        name="attend",
    )(sec, *far)


def quarter_kernel(kv_ref, mine_ref, got_ref, *out_refs):
    count = len(out_refs)
    rows = mine_ref.shape[0] // count
    for step, out_ref in enumerate(out_refs):
        at = pl.ds(pl.multiple_of(lax.rem(kv_ref[0] + step, count) * rows, rows), rows)
        out_ref[...] = (mine_ref[at, :].astype(F32) + got_ref[at, :].astype(F32)).astype(BF16)


def quarter(kv, mine, got, count):
    rows, width = mine.shape
    out = jax.ShapeDtypeStruct((rows // count, width), BF16)
    return pl.pallas_call(
        quarter_kernel,
        in_specs=[whole(SMEM), whole(), whole()],
        out_specs=[whole()] * count,
        out_shape=[out] * count,
        compiler_params=pltpu.CompilerParams(vmem_limit_bytes=4 * MIB),
        name="quarter",
    )(kv, mine, got)


def route_kernel(ids_ref, slots_ref, *refs):
    part_refs, (residual_ref, gain_ref, stream_hbm, out_ref, wide_ref, stream_ref, sem) = refs[:-7], refs[-7:]
    rows, width = residual_ref.shape
    pieces = width // LANES
    top = ids_ref.shape[0]
    stride = pieces + GAP
    out_ref[...] = jnp.zeros_like(out_ref)
    proj = part_refs[0][...].astype(F32)
    for part_ref in part_refs[1:]:
        proj = proj + part_ref[...].astype(F32)
    stream = (residual_ref[...].astype(F32) + proj).astype(BF16)
    stream_ref[...] = stream
    leave = pltpu.make_async_copy(stream_ref, stream_hbm, sem)
    leave.start()
    widened = stream.astype(F32)
    mean_square = jnp.mean(widened * widened, axis=-1, keepdims=True)
    normed = widened * lax.rsqrt(mean_square + 1e-06) * gain_ref[...]
    for t in range(0, rows, 8):
        for s in range(pieces):
            wide_ref[pl.ds(t * stride + s, 8, stride=stride), :] = normed[t : t + 8, s * LANES : (s + 1) * LANES]

    def one(t, carry):
        row = wide_ref[pl.ds(t * stride, pieces), :].astype(BF16)
        for k in range(top):
            out_ref[ids_ref[k, t], slots_ref[k, t]] = row
        return carry

    lax.fori_loop(0, rows, one, 0, unroll=4)
    leave.wait()


def route(ids, slots, parts, residual, gain, expert_count, capacity):
    rows, width = residual.shape
    pieces = width // LANES
    return pl.pallas_call(
        route_kernel,
        in_specs=[whole(SMEM), whole(SMEM)] + [whole()] * (len(parts) + 2),
        out_specs=[whole(pl.ANY), whole()],
        out_shape=[
            jax.ShapeDtypeStruct((rows, width), BF16),
            jax.ShapeDtypeStruct((expert_count, capacity, pieces, LANES), BF16),
        ],
        scratch_shapes=[
            pltpu.VMEM((rows * (pieces + GAP) + SPARE, LANES), F32),
            pltpu.VMEM((rows, width), BF16),
            pltpu.SemaphoreType.DMA,
        ],
        compiler_params=pltpu.CompilerParams(vmem_limit_bytes=4 * MIB),
        name="route",
    )(ids, slots, *parts, residual, gain)


def load_kernel(*refs):
    count = len(refs) // 2
    sems = refs[-1]
    copies = [pltpu.make_async_copy(refs[i], refs[count + i], sems.at[i]) for i in range(count)]
    for copy in copies:
        copy.start()
    for copy in copies:
        copy.wait()


def load(weights, tables):
    size = sum(w.size * 2 for w in weights)
    arrays = [*weights, *tables]
    out = pl.pallas_call(
        load_kernel,
        in_specs=[whole(pltpu.HBM)] * len(arrays),
        out_specs=[whole()] * len(weights) + [whole(SMEM)] * len(tables),
        out_shape=[pltpu.VMEM(w.shape, w.dtype) for w in weights] + [pltpu.SMEM(t.shape, t.dtype) for t in tables],
        scratch_shapes=[pltpu.SemaphoreType.DMA((len(arrays),))],
        compiler_params=pltpu.CompilerParams(vmem_limit_bytes=2 * MIB),
        cost_estimate=pl.CostEstimate(flops=0, bytes_accessed=2 * size, transcendentals=0),
        name="load",
    )(*[pltpu.with_memory_space_constraint(a, pltpu.HBM) for a in arrays])
    return out[: len(weights)], out[len(weights) :]


def expert_kernel(x_ref, wg_ref, wu_ref, wd_hbm, out_ref, wide_ref, flat_ref, hidden_ref, wd_ref, sem):
    rows, pieces, _ = x_ref.shape
    hidden_width = wg_ref.shape[1]
    width = pieces * LANES
    stride = pieces + GAP
    ncols = 256
    dcols = 1024
    group = 16
    down_copy = pltpu.make_async_copy(wd_hbm, wd_ref, sem)
    down_copy.start()

    def spread(i, carry):
        base = pl.multiple_of(i * group, group)
        for r in range(group):
            wide_ref[pl.ds(r * stride, pieces), :] = x_ref[base + r].astype(F32)
        for s in range(pieces):
            low = wide_ref[pl.ds(s, 8, stride=stride), :]
            high = wide_ref[pl.ds(8 * stride + s, 8, stride=stride), :]
            flat_ref[pl.ds(base, group), pl.ds(s * LANES, LANES)] = jnp.concatenate([low, high], axis=0).astype(BF16)
        return carry

    lax.fori_loop(0, rows // group, spread, 0)

    for n in range(hidden_width // ncols):
        at = pl.ds(n * ncols, ncols)
        gate = jnp.dot(flat_ref[...], wg_ref[:, at], preferred_element_type=F32)
        up = jnp.dot(flat_ref[...], wu_ref[:, at], preferred_element_type=F32)
        hidden_ref[:, at] = (gate / (1.0 + jnp.exp(-gate)) * up).astype(BF16)

    down_copy.wait()
    for n in range(width // dcols):
        done = jnp.dot(hidden_ref[...], wd_ref[:, pl.ds(n * dcols, dcols)], preferred_element_type=F32)
        for r in range(0, rows, 8):
            for s in range(dcols // LANES):
                wide_ref[pl.ds(r * stride + n * (dcols // LANES) + s, 8, stride=stride), :] = done[
                    r : r + 8, s * LANES : (s + 1) * LANES
                ]

    def narrow(i, carry):
        base = pl.multiple_of(i * group, group)
        for r in range(group):
            out_ref[base + r] = wide_ref[pl.ds((base + r) * stride, pieces), :].astype(BF16)
        return carry

    lax.fori_loop(0, rows // group, narrow, 0)


def expert(x, wg, wu, wd):
    rows, pieces, _ = x.shape
    width, hidden_width = wg.shape
    near = [pltpu.with_memory_space_constraint(w, pltpu.VMEM) for w in (wg, wu)]
    return pl.pallas_call(
        expert_kernel,
        in_specs=[whole()] * 3 + [whole(pltpu.HBM)],
        out_specs=whole(),
        out_shape=jax.ShapeDtypeStruct(x.shape, BF16),
        scratch_shapes=[
            pltpu.VMEM((rows * (pieces + GAP) + SPARE, LANES), F32),
            pltpu.VMEM((rows, width), BF16),
            pltpu.VMEM((rows, hidden_width), BF16),
            pltpu.VMEM(wd.shape, BF16),
            pltpu.SemaphoreType.DMA,
        ],
        compiler_params=pltpu.CompilerParams(vmem_limit_bytes=20 * MIB),
        name="expert",
    )(x, *near, pltpu.with_memory_space_constraint(wd, pltpu.HBM))


def combine_kernel(ids_ref, slots_ref, probs_ref, rows_ref, out_ref, wide_ref):
    rows, width = out_ref.shape
    pieces = width // LANES
    top = ids_ref.shape[0]
    stride = pieces + GAP

    def one(t, carry):
        total = None
        for k in range(top):
            term = rows_ref[ids_ref[k, t], slots_ref[k, t]].astype(F32) * probs_ref[k, t]
            total = term if total is None else total + term
        wide_ref[pl.ds(t * stride, pieces), :] = total
        return carry

    lax.fori_loop(0, rows, one, 0, unroll=4)
    for s in range(pieces):
        low = wide_ref[pl.ds(s, 8, stride=stride), :]
        high = wide_ref[pl.ds(8 * stride + s, 8, stride=stride), :]
        out_ref[:, pl.ds(s * LANES, LANES)] = jnp.concatenate([low, high], axis=0).astype(BF16)


def combine(ids, slots, probs, returned, width):
    rows = ids.shape[1]
    return pl.pallas_call(
        combine_kernel,
        in_specs=[whole(SMEM)] * 3 + [whole()],
        out_specs=whole(),
        out_shape=jax.ShapeDtypeStruct((rows, width), BF16),
        scratch_shapes=[pltpu.VMEM((rows * (width // LANES + GAP) + SPARE, LANES), F32)],
        compiler_params=pltpu.CompilerParams(vmem_limit_bytes=4 * MIB),
        name="combine",
    )(ids, slots, probs, returned)


def on_device(
    queries,
    key_cache,
    value_cache,
    new_keys,
    new_values,
    lengths,
    out_proj,
    residual,
    norm_gain,
    expert_ids,
    expert_slots,
    gate_probs,
    w_gate,
    w_up,
    w_down,
):
    row_count = queries.shape[0]
    width = out_proj.shape[1]
    pieces = width // LANES
    sec_count, group_count = lax.axis_size("sec"), lax.axis_size("kv")
    expert_count = sec_count * lax.axis_size("req") * group_count
    row_share, top_count = expert_ids.shape
    capacity = top_count * row_share // expert_count + 1
    sec = lax.axis_index("sec").astype(jnp.int32).reshape(1)
    kv = lax.axis_index("kv").astype(jnp.int32).reshape(1)

    theirs, mine = attend(
        sec,
        lengths.reshape(1, row_count),
        queries,
        key_cache.reshape(-1, LANES),
        value_cache.reshape(-1, LANES),
        new_keys.reshape(row_count, LANES),
        new_values.reshape(row_count, LANES),
        out_proj,
    )
    got = lax.ppermute(theirs, "sec", [(i, 1 - i) for i in range(sec_count)])
    quarters = quarter(kv, mine, got, group_count)
    parts = [quarters[0]]
    for s in sorted(range(1, group_count), key=lambda s: min(s, group_count - s)):
        parts.append(lax.ppermute(quarters[s], "kv", [(i, (i + s) % group_count) for i in range(group_count)]))
    weights, tables = load((w_gate[0], w_up[0]), (expert_ids.T, expert_slots.T, gate_probs.T))
    ids, slots, probs = tables
    stream, outgoing = route(ids, slots, parts, residual, norm_gain.reshape(1, width), expert_count, capacity)

    def exchange(rows):
        sent = rows.reshape(expert_count, capacity * pieces, LANES)
        return lax.all_to_all(sent, ("sec", "req", "kv"), split_axis=0, concat_axis=0, tiled=True)

    outgoing, *weights = lax.optimization_barrier((outgoing, *weights))
    arrived = exchange(outgoing).reshape(expert_count * capacity, pieces, LANES)
    finished = expert(arrived, *weights, w_down[0])
    returned = exchange(finished).reshape(expert_count, capacity, pieces, LANES)
    moe_out = combine(ids, slots, probs, returned, width)
    return (stream, moe_out)


def solution(mesh):
    return jax.shard_map(
        on_device,
        mesh=mesh,
        in_specs=(
            P("req", ("kv", "sec")),
            P("req", "kv", None, None),
            P("req", "kv", None, None),
            P("req", "kv", None),
            P("req", "kv", None),
            P("req"),
            P(("kv", "sec"), None),
            P(("req", "sec", "kv"), None),
            P(),
            P(("req", "sec", "kv"), None),
            P(("req", "sec", "kv"), None),
            P(("req", "sec", "kv"), None),
            P(("sec", "req", "kv"), None, None),
            P(("sec", "req", "kv"), None, None),
            P(("sec", "req", "kv"), None, None),
        ),
        out_specs=(P(("req", "sec", "kv"), None), P(("req", "sec", "kv"), None)),
        check_vma=False,
    )
```

```python
import math

import jax
import jax.numpy as jnp
from jax import lax
from jax.experimental import pallas as pl
from jax.experimental.pallas import tpu as pltpu
from jax.sharding import PartitionSpec as P

LANES = 128
F32 = jnp.float32
BF16 = jnp.bfloat16
MIB = 1 << 20

GAP = 1
SPARE = 40

VMEM = pltpu.VMEM
SMEM = pltpu.SMEM


def whole(space=VMEM):
    return pl.BlockSpec(memory_space=space)


BLOCKS = 4


def attend_kernel(
    sec_ref,
    kv_ref,
    len_hbm,
    q_hbm,
    kc_hbm,
    vc_hbm,
    nk_hbm,
    nv_hbm,
    wo_hbm,
    theirs_ref,
    mine_ref,
    len_ref,
    q_ref,
    kc_ref,
    vc_ref,
    nk_ref,
    nv_ref,
    wo_ref,
    attn_ref,
    sems,
):
    rows, head_width = q_ref.shape
    heads = head_width // LANES
    positions = kc_ref.shape[0] // rows
    group = 8
    to_exponent = math.log2(math.e) / LANES**0.5
    half = rows // 2
    far = half // BLOCKS

    small = [
        pltpu.make_async_copy(source, target, sems.at[i])
        for i, (source, target) in enumerate(((len_hbm, len_ref), (q_hbm, q_ref), (nk_hbm, nk_ref), (nv_hbm, nv_ref)))
    ]
    key_copy = pltpu.make_async_copy(kc_hbm, kc_ref, sems.at[4])
    value_copy = pltpu.make_async_copy(vc_hbm, vc_ref, sems.at[5])
    wo_copy = pltpu.make_async_copy(wo_hbm, wo_ref, sems.at[6])
    for copy in (*small, key_copy, value_copy, wo_copy):
        copy.start()

    for copy in small:
        copy.wait()
    r = lax.broadcasted_iota(jnp.int32, (rows, rows), 0)
    c = lax.broadcasted_iota(jnp.int32, (rows, rows), 1)
    lengths = jnp.sum(jnp.where(r == c, len_ref[...], 0).astype(F32), axis=1, keepdims=True)
    span = group * positions
    row_token = lax.broadcasted_iota(jnp.int32, (heads * group, span), 0) % group
    column = lax.broadcasted_iota(jnp.int32, (heads * group, span), 1)
    own_column = column - row_token * positions
    own_position = jnp.where(own_column >= 0, own_column, positions).astype(F32)

    def per_head(rows_of_group):
        return jnp.concatenate([rows_of_group] * heads, axis=0)

    def group_rows(ref, g):
        pair = ref[pl.ds(g // 2 * 2 * group, 2 * group), :].astype(F32)
        return pair[g % 2 * group : (g % 2 + 1) * group]

    groups = rows // group
    scores, own_scores, raised, own_raised, outs = [], [], [], [], []
    key_copy.wait()
    for g in range(groups):
        q_rows = group_rows(q_ref, g)
        q = jnp.concatenate([q_rows[:, h * LANES : (h + 1) * LANES] for h in range(heads)], axis=0)
        keys = kc_ref[pl.ds(g * span, span), :]
        score = lax.dot_general(q.astype(BF16), keys, (((1,), (1,)), ((), ())), preferred_element_type=F32)
        scores.append(jnp.where(own_position < per_head(lengths[g * group : (g + 1) * group]), score, -jnp.inf))
        own_scores.append(jnp.sum(q * per_head(group_rows(nk_ref, g)), axis=1, keepdims=True))
    for score, own_score in zip(scores, own_scores):
        highest = jnp.maximum(jnp.max(score, axis=1, keepdims=True), own_score)
        raised.append(jnp.exp2((score - highest) * to_exponent))
        own_raised.append(jnp.exp2((own_score - highest) * to_exponent))
    value_copy.wait()
    for g in range(groups):
        inverse = 1.0 / (jnp.sum(raised[g], axis=1, keepdims=True) + own_raised[g])
        values = vc_ref[pl.ds(g * span, span), :]
        out = jnp.dot(raised[g].astype(BF16), values, preferred_element_type=F32)
        outs.append((out + own_raised[g] * per_head(group_rows(nv_ref, g))) * inverse)
    for g in range(0, groups, 2):
        block, blocks = g * group // far, half // far
        way = 1 - 2 * (block // blocks)
        turned = lax.rem(way * (block % blocks - kv_ref[0]) + blocks + blocks // 2, blocks)
        side = lax.rem(block // blocks + 1 - sec_ref[0], 2)
        place = pl.multiple_of(side * half + turned * far, 2 * group)
        for h in range(heads):
            pair = [outs[g + j][h * group : (h + 1) * group] for j in range(2)]
            attn_ref[pl.ds(place, 2 * group), pl.ds(h * LANES, LANES)] = jnp.concatenate(pair, axis=0).astype(BF16)

    wo_copy.wait()
    proj = jnp.dot(attn_ref[...], wo_ref[...], preferred_element_type=F32)
    theirs_ref[...] = proj[:half].astype(BF16)
    mine_ref[...] = proj[half:].astype(BF16)


def attend(sec, kv, lengths, q, kc, vc, nk, nv, wo):
    rows, head_width = q.shape
    width = wo.shape[1]
    out = [jax.ShapeDtypeStruct((rows // 2, width), BF16)]
    far = [pltpu.with_memory_space_constraint(a, pltpu.HBM) for a in (lengths, q, kc, vc, nk, nv, wo)]
    return pl.pallas_call(
        attend_kernel,
        in_specs=[whole(SMEM)] * 2 + [whole(pltpu.HBM)] * 7,
        out_specs=[whole()] * 2,
        out_shape=out * 2,
        scratch_shapes=[pltpu.VMEM(a.shape, a.dtype) for a in (lengths, q, kc, vc, nk, nv)]
        + [
            pltpu.VMEM(wo.shape, BF16),
            pltpu.VMEM((rows, head_width), BF16),
            pltpu.SemaphoreType.DMA((7,)),
        ],
        compiler_params=pltpu.CompilerParams(vmem_limit_bytes=14 * MIB),
        name="attend",
    )(sec, kv, *far)


def join_kernel(mine_ref, got_ref, *out_refs):
    rows = out_refs[0].shape[0]
    for i, out_ref in enumerate(out_refs):
        at = pl.ds(i * rows, rows)
        out_ref[...] = (mine_ref[at, :].astype(F32) + got_ref[at, :].astype(F32)).astype(BF16)


def join(mine, got, parts):
    rows, width = mine.shape
    out = jax.ShapeDtypeStruct((rows // parts, width), BF16)
    return pl.pallas_call(
        join_kernel,
        in_specs=[whole(), whole()],
        out_specs=[whole()] * parts,
        out_shape=[out] * parts,
        compiler_params=pltpu.CompilerParams(vmem_limit_bytes=4 * MIB),
        name="join",
    )(mine, got)


def route_kernel(ids_ref, slots_ref, *refs):
    part_refs, (residual_ref, gain_ref, stream_hbm, out_ref, wide_ref, stream_ref, sem) = refs[:-7], refs[-7:]
    rows, width = residual_ref.shape
    pieces = width // LANES
    top = ids_ref.shape[0]
    stride = pieces + GAP
    out_ref[...] = jnp.zeros_like(out_ref)
    proj = part_refs[0][...].astype(F32)
    for part_ref in part_refs[1:]:
        proj = proj + part_ref[...].astype(F32)
    stream = (residual_ref[...].astype(F32) + proj).astype(BF16)
    stream_ref[...] = stream
    leave = pltpu.make_async_copy(stream_ref, stream_hbm, sem)
    leave.start()
    widened = stream.astype(F32)
    mean_square = jnp.mean(widened * widened, axis=-1, keepdims=True)
    normed = widened * lax.rsqrt(mean_square + 1e-06) * gain_ref[...]
    for t in range(0, rows, 8):
        for s in range(pieces):
            wide_ref[pl.ds(t * stride + s, 8, stride=stride), :] = normed[t : t + 8, s * LANES : (s + 1) * LANES]

    def one(t, carry):
        row = wide_ref[pl.ds(t * stride, pieces), :].astype(BF16)
        for k in range(top):
            out_ref[ids_ref[k, t], slots_ref[k, t]] = row
        return carry

    lax.fori_loop(0, rows, one, 0, unroll=4)
    leave.wait()


def route(ids, slots, parts, residual, gain, expert_count, capacity):
    rows, width = residual.shape
    pieces = width // LANES
    return pl.pallas_call(
        route_kernel,
        in_specs=[whole(SMEM), whole(SMEM)] + [whole()] * (len(parts) + 2),
        out_specs=[whole(pl.ANY), whole()],
        out_shape=[
            jax.ShapeDtypeStruct((rows, width), BF16),
            jax.ShapeDtypeStruct((expert_count, capacity, pieces, LANES), BF16),
        ],
        scratch_shapes=[
            pltpu.VMEM((rows * (pieces + GAP) + SPARE, LANES), F32),
            pltpu.VMEM((rows, width), BF16),
            pltpu.SemaphoreType.DMA,
        ],
        compiler_params=pltpu.CompilerParams(vmem_limit_bytes=4 * MIB),
        name="route",
    )(ids, slots, *parts, residual, gain)


def load_kernel(*refs):
    count = len(refs) // 2
    sems = refs[-1]
    copies = [pltpu.make_async_copy(refs[i], refs[count + i], sems.at[i]) for i in range(count)]
    for copy in copies:
        copy.start()
    for copy in copies:
        copy.wait()


def load(weights, tables):
    size = sum(w.size * 2 for w in weights)
    arrays = [*weights, *tables]
    out = pl.pallas_call(
        load_kernel,
        in_specs=[whole(pltpu.HBM)] * len(arrays),
        out_specs=[whole()] * len(weights) + [whole(SMEM)] * len(tables),
        out_shape=[pltpu.VMEM(w.shape, w.dtype) for w in weights] + [pltpu.SMEM(t.shape, t.dtype) for t in tables],
        scratch_shapes=[pltpu.SemaphoreType.DMA((len(arrays),))],
        compiler_params=pltpu.CompilerParams(vmem_limit_bytes=2 * MIB),
        cost_estimate=pl.CostEstimate(flops=0, bytes_accessed=2 * size, transcendentals=0),
        name="load",
    )(*[pltpu.with_memory_space_constraint(a, pltpu.HBM) for a in arrays])
    return out[: len(weights)], out[len(weights) :]


def expert_kernel(x_ref, wg_ref, wu_ref, wd_hbm, out_ref, wide_ref, flat_ref, hidden_ref, wd_ref, sem):
    rows, pieces, _ = x_ref.shape
    hidden_width = wg_ref.shape[1]
    width = pieces * LANES
    stride = pieces + GAP
    ncols = 256
    dcols = 1024
    group = 16
    down_copy = pltpu.make_async_copy(wd_hbm, wd_ref, sem)
    down_copy.start()

    def spread(i, carry):
        base = pl.multiple_of(i * group, group)
        for r in range(group):
            wide_ref[pl.ds(r * stride, pieces), :] = x_ref[base + r].astype(F32)
        for s in range(pieces):
            low = wide_ref[pl.ds(s, 8, stride=stride), :]
            high = wide_ref[pl.ds(8 * stride + s, 8, stride=stride), :]
            flat_ref[pl.ds(base, group), pl.ds(s * LANES, LANES)] = jnp.concatenate([low, high], axis=0).astype(BF16)
        return carry

    lax.fori_loop(0, rows // group, spread, 0)

    for n in range(hidden_width // ncols):
        at = pl.ds(n * ncols, ncols)
        gate = jnp.dot(flat_ref[...], wg_ref[:, at], preferred_element_type=F32)
        up = jnp.dot(flat_ref[...], wu_ref[:, at], preferred_element_type=F32)
        hidden_ref[:, at] = (gate / (1.0 + jnp.exp(-gate)) * up).astype(BF16)

    down_copy.wait()
    for n in range(width // dcols):
        done = jnp.dot(hidden_ref[...], wd_ref[:, pl.ds(n * dcols, dcols)], preferred_element_type=F32)
        for r in range(0, rows, 8):
            for s in range(dcols // LANES):
                wide_ref[pl.ds(r * stride + n * (dcols // LANES) + s, 8, stride=stride), :] = done[
                    r : r + 8, s * LANES : (s + 1) * LANES
                ]

    def narrow(i, carry):
        base = pl.multiple_of(i * group, group)
        for r in range(group):
            out_ref[base + r] = wide_ref[pl.ds((base + r) * stride, pieces), :].astype(BF16)
        return carry

    lax.fori_loop(0, rows // group, narrow, 0)


def expert(x, wg, wu, wd):
    rows, pieces, _ = x.shape
    width, hidden_width = wg.shape
    near = [pltpu.with_memory_space_constraint(w, pltpu.VMEM) for w in (wg, wu)]
    return pl.pallas_call(
        expert_kernel,
        in_specs=[whole()] * 3 + [whole(pltpu.HBM)],
        out_specs=whole(),
        out_shape=jax.ShapeDtypeStruct(x.shape, BF16),
        scratch_shapes=[
            pltpu.VMEM((rows * (pieces + GAP) + SPARE, LANES), F32),
            pltpu.VMEM((rows, width), BF16),
            pltpu.VMEM((rows, hidden_width), BF16),
            pltpu.VMEM(wd.shape, BF16),
            pltpu.SemaphoreType.DMA,
        ],
        compiler_params=pltpu.CompilerParams(vmem_limit_bytes=20 * MIB),
        name="expert",
    )(x, *near, pltpu.with_memory_space_constraint(wd, pltpu.HBM))


def combine_kernel(ids_ref, slots_ref, probs_ref, rows_ref, out_ref, wide_ref):
    rows, width = out_ref.shape
    pieces = width // LANES
    top = ids_ref.shape[0]
    stride = pieces + GAP

    def one(t, carry):
        total = None
        for k in range(top):
            term = rows_ref[ids_ref[k, t], slots_ref[k, t]].astype(F32) * probs_ref[k, t]
            total = term if total is None else total + term
        wide_ref[pl.ds(t * stride, pieces), :] = total
        return carry

    lax.fori_loop(0, rows, one, 0, unroll=4)
    for s in range(pieces):
        low = wide_ref[pl.ds(s, 8, stride=stride), :]
        high = wide_ref[pl.ds(8 * stride + s, 8, stride=stride), :]
        out_ref[:, pl.ds(s * LANES, LANES)] = jnp.concatenate([low, high], axis=0).astype(BF16)


def combine(ids, slots, probs, returned, width):
    rows = ids.shape[1]
    return pl.pallas_call(
        combine_kernel,
        in_specs=[whole(SMEM)] * 3 + [whole()],
        out_specs=whole(),
        out_shape=jax.ShapeDtypeStruct((rows, width), BF16),
        scratch_shapes=[pltpu.VMEM((rows * (width // LANES + GAP) + SPARE, LANES), F32)],
        compiler_params=pltpu.CompilerParams(vmem_limit_bytes=4 * MIB),
        name="combine",
    )(ids, slots, probs, returned)


def on_device(
    queries,
    key_cache,
    value_cache,
    new_keys,
    new_values,
    lengths,
    out_proj,
    residual,
    norm_gain,
    expert_ids,
    expert_slots,
    gate_probs,
    w_gate,
    w_up,
    w_down,
):
    row_count = queries.shape[0]
    width = out_proj.shape[1]
    pieces = width // LANES
    sec_count, group_count = lax.axis_size("sec"), lax.axis_size("kv")
    expert_count = sec_count * lax.axis_size("req") * group_count
    row_share, top_count = expert_ids.shape
    capacity = top_count * row_share // expert_count + 1
    sec = lax.axis_index("sec").astype(jnp.int32).reshape(1)
    kv = lax.axis_index("kv").astype(jnp.int32).reshape(1)

    theirs, mine = attend(
        sec,
        kv,
        lengths.reshape(1, row_count),
        queries,
        key_cache.reshape(-1, LANES),
        value_cache.reshape(-1, LANES),
        new_keys.reshape(row_count, LANES),
        new_values.reshape(row_count, LANES),
        out_proj,
    )

    def other_core(x):
        return lax.ppermute(x, "sec", [(i, 1 - i) for i in range(sec_count)])

    def along(x, step):
        pairs = [
            (c * group_count + i, c * group_count + (i + step * (1 - 2 * c)) % group_count)
            for c in range(sec_count)
            for i in range(group_count)
        ]
        return lax.ppermute(x, ("sec", "kv"), pairs)

    far, before, keep, after = join(mine, other_core(theirs), group_count)
    parts = [keep, along(after, 1), along(before, -1), along(far, 2)]
    weights, tables = load((w_gate[0], w_up[0]), (expert_ids.T, expert_slots.T, gate_probs.T))
    ids, slots, probs = tables
    stream, outgoing = route(ids, slots, parts, residual, norm_gain.reshape(1, width), expert_count, capacity)

    def exchange(rows):
        sent = rows.reshape(expert_count, capacity * pieces, LANES)
        return lax.all_to_all(sent, ("sec", "req", "kv"), split_axis=0, concat_axis=0, tiled=True)

    outgoing, *weights = lax.optimization_barrier((outgoing, *weights))
    arrived = exchange(outgoing).reshape(expert_count * capacity, pieces, LANES)
    finished = expert(arrived, *weights, w_down[0])
    returned = exchange(finished).reshape(expert_count, capacity, pieces, LANES)
    moe_out = combine(ids, slots, probs, returned, width)
    return (stream, moe_out)


def solution(mesh):
    return jax.shard_map(
        on_device,
        mesh=mesh,
        in_specs=(
            P("req", ("kv", "sec")),
            P("req", "kv", None, None),
            P("req", "kv", None, None),
            P("req", "kv", None),
            P("req", "kv", None),
            P("req"),
            P(("kv", "sec"), None),
            P(("req", "sec", "kv"), None),
            P(),
            P(("req", "sec", "kv"), None),
            P(("req", "sec", "kv"), None),
            P(("req", "sec", "kv"), None),
            P(("sec", "req", "kv"), None, None),
            P(("sec", "req", "kv"), None, None),
            P(("sec", "req", "kv"), None, None),
        ),
        out_specs=(P(("req", "sec", "kv"), None), P(("req", "sec", "kv"), None)),
        check_vma=False,
    )
```

```python
import math

import jax
import jax.numpy as jnp
from jax import lax
from jax.experimental import pallas as pl
from jax.experimental.pallas import tpu as pltpu
from jax.sharding import PartitionSpec as P

LANES = 128
F32 = jnp.float32
BF16 = jnp.bfloat16
MIB = 1 << 20

GAP = 1
SPARE = 40

VMEM = pltpu.VMEM
SMEM = pltpu.SMEM


def whole(space=VMEM):
    return pl.BlockSpec(memory_space=space)


BLOCKS = 4


def attend_kernel(
    sec_ref,
    kv_ref,
    len_hbm,
    q_hbm,
    kc_hbm,
    vc_hbm,
    nk_hbm,
    nv_hbm,
    wo_hbm,
    theirs_ref,
    mine_ref,
    len_ref,
    q_ref,
    kc_ref,
    vc_ref,
    nk_ref,
    nv_ref,
    wo_ref,
    attn_ref,
    sems,
):
    rows, head_width = q_ref.shape
    heads = head_width // LANES
    positions = kc_ref.shape[0] // rows
    group = 8
    to_exponent = math.log2(math.e) / LANES**0.5
    half = rows // 2
    far = half // BLOCKS

    small = [
        pltpu.make_async_copy(source, target, sems.at[i])
        for i, (source, target) in enumerate(((len_hbm, len_ref), (q_hbm, q_ref), (nk_hbm, nk_ref), (nv_hbm, nv_ref)))
    ]
    key_copy = pltpu.make_async_copy(kc_hbm, kc_ref, sems.at[4])
    value_copy = pltpu.make_async_copy(vc_hbm, vc_ref, sems.at[5])
    wo_copy = pltpu.make_async_copy(wo_hbm, wo_ref, sems.at[6])
    for copy in (*small, key_copy, value_copy, wo_copy):
        copy.start()

    for copy in small:
        copy.wait()
    r = lax.broadcasted_iota(jnp.int32, (rows, rows), 0)
    c = lax.broadcasted_iota(jnp.int32, (rows, rows), 1)
    lengths = jnp.sum(jnp.where(r == c, len_ref[...], 0).astype(F32), axis=1, keepdims=True)
    span = group * positions
    row_token = lax.broadcasted_iota(jnp.int32, (heads * group, span), 0) % group
    column = lax.broadcasted_iota(jnp.int32, (heads * group, span), 1)
    own_column = column - row_token * positions
    own_position = jnp.where(own_column >= 0, own_column, positions).astype(F32)

    def per_head(rows_of_group):
        return jnp.concatenate([rows_of_group] * heads, axis=0)

    def group_rows(ref, g):
        pair = ref[pl.ds(g // 2 * 2 * group, 2 * group), :].astype(F32)
        return pair[g % 2 * group : (g % 2 + 1) * group]

    groups = rows // group
    scores, own_scores, raised, own_raised, outs = [], [], [], [], []
    key_copy.wait()
    for g in range(groups):
        q_rows = group_rows(q_ref, g)
        q = jnp.concatenate([q_rows[:, h * LANES : (h + 1) * LANES] for h in range(heads)], axis=0)
        keys = kc_ref[pl.ds(g * span, span), :]
        score = lax.dot_general(q.astype(BF16), keys, (((1,), (1,)), ((), ())), preferred_element_type=F32)
        scores.append(jnp.where(own_position < per_head(lengths[g * group : (g + 1) * group]), score, -jnp.inf))
        own_scores.append(jnp.sum(q * per_head(group_rows(nk_ref, g)), axis=1, keepdims=True))
    for score, own_score in zip(scores, own_scores):
        highest = jnp.maximum(jnp.max(score, axis=1, keepdims=True), own_score)
        raised.append(jnp.exp2((score - highest) * to_exponent))
        own_raised.append(jnp.exp2((own_score - highest) * to_exponent))
    value_copy.wait()
    for g in range(groups):
        inverse = 1.0 / (jnp.sum(raised[g], axis=1, keepdims=True) + own_raised[g])
        values = vc_ref[pl.ds(g * span, span), :]
        out = jnp.dot(raised[g].astype(BF16), values, preferred_element_type=F32)
        outs.append((out + own_raised[g] * per_head(group_rows(nv_ref, g))) * inverse)
    for g in range(0, groups, 2):
        block, blocks = g * group // far, half // far
        way = 1 - 2 * (block // blocks)
        turned = lax.rem(way * (block % blocks - kv_ref[0]) + blocks + blocks // 2, blocks)
        side = lax.rem(block // blocks + 1 - sec_ref[0], 2)
        place = pl.multiple_of(side * half + turned * far, 2 * group)
        for h in range(heads):
            pair = [outs[g + j][h * group : (h + 1) * group] for j in range(2)]
            attn_ref[pl.ds(place, 2 * group), pl.ds(h * LANES, LANES)] = jnp.concatenate(pair, axis=0).astype(BF16)

    wo_copy.wait()
    proj = jnp.dot(attn_ref[...], wo_ref[...], preferred_element_type=F32)
    theirs_ref[...] = proj[:half].astype(BF16)
    mine_ref[...] = proj[half:].astype(BF16)


def attend(sec, kv, lengths, q, kc, vc, nk, nv, wo):
    rows, head_width = q.shape
    width = wo.shape[1]
    out = [jax.ShapeDtypeStruct((rows // 2, width), BF16)]
    far = [pltpu.with_memory_space_constraint(a, pltpu.HBM) for a in (lengths, q, kc, vc, nk, nv, wo)]
    return pl.pallas_call(
        attend_kernel,
        in_specs=[whole(SMEM)] * 2 + [whole(pltpu.HBM)] * 7,
        out_specs=[whole()] * 2,
        out_shape=out * 2,
        scratch_shapes=[pltpu.VMEM(a.shape, a.dtype) for a in (lengths, q, kc, vc, nk, nv)]
        + [
            pltpu.VMEM(wo.shape, BF16),
            pltpu.VMEM((rows, head_width), BF16),
            pltpu.SemaphoreType.DMA((7,)),
        ],
        compiler_params=pltpu.CompilerParams(vmem_limit_bytes=14 * MIB),
        name="attend",
    )(sec, kv, *far)


def join_kernel(mine_ref, got_ref, *out_refs):
    rows = out_refs[0].shape[0]
    for i, out_ref in enumerate(out_refs):
        at = pl.ds(i * rows, rows)
        out_ref[...] = (mine_ref[at, :].astype(F32) + got_ref[at, :].astype(F32)).astype(BF16)


def join(mine, got, parts):
    rows, width = mine.shape
    out = jax.ShapeDtypeStruct((rows // parts, width), BF16)
    return pl.pallas_call(
        join_kernel,
        in_specs=[whole(), whole()],
        out_specs=[whole()] * parts,
        out_shape=[out] * parts,
        compiler_params=pltpu.CompilerParams(vmem_limit_bytes=4 * MIB),
        name="join",
    )(mine, got)


def route_kernel(ids_ref, slots_ref, *refs):
    part_refs, (residual_ref, gain_ref, stream_hbm, out_ref, wide_ref, stream_ref, sem) = refs[:-7], refs[-7:]
    rows, width = residual_ref.shape
    pieces = width // LANES
    top = ids_ref.shape[0]
    stride = pieces + GAP
    out_ref[...] = jnp.zeros_like(out_ref)
    proj = part_refs[0][...].astype(F32)
    for part_ref in part_refs[1:]:
        proj = proj + part_ref[...].astype(F32)
    stream = (residual_ref[...].astype(F32) + proj).astype(BF16)
    stream_ref[...] = stream
    leave = pltpu.make_async_copy(stream_ref, stream_hbm, sem)
    leave.start()
    widened = stream.astype(F32)
    mean_square = jnp.mean(widened * widened, axis=-1, keepdims=True)
    normed = widened * lax.rsqrt(mean_square + 1e-06) * gain_ref[...]
    for t in range(0, rows, 8):
        for s in range(pieces):
            wide_ref[pl.ds(t * stride + s, 8, stride=stride), :] = normed[t : t + 8, s * LANES : (s + 1) * LANES]

    def one(t, carry):
        row = wide_ref[pl.ds(t * stride, pieces), :].astype(BF16)
        for k in range(top):
            out_ref[ids_ref[k, t], slots_ref[k, t]] = row
        return carry

    lax.fori_loop(0, rows, one, 0, unroll=4)
    leave.wait()


def route(ids, slots, parts, residual, gain, expert_count, capacity):
    rows, width = residual.shape
    pieces = width // LANES
    return pl.pallas_call(
        route_kernel,
        in_specs=[whole(SMEM), whole(SMEM)] + [whole()] * (len(parts) + 2),
        out_specs=[whole(pl.ANY), whole()],
        out_shape=[
            jax.ShapeDtypeStruct((rows, width), BF16),
            jax.ShapeDtypeStruct((expert_count, capacity, pieces, LANES), BF16),
        ],
        scratch_shapes=[
            pltpu.VMEM((rows * (pieces + GAP) + SPARE, LANES), F32),
            pltpu.VMEM((rows, width), BF16),
            pltpu.SemaphoreType.DMA,
        ],
        compiler_params=pltpu.CompilerParams(vmem_limit_bytes=4 * MIB),
        name="route",
    )(ids, slots, *parts, residual, gain)


def load_kernel(*refs):
    count = len(refs) // 2
    sems = refs[-1]
    copies = [pltpu.make_async_copy(refs[i], refs[count + i], sems.at[i]) for i in range(count)]
    for copy in copies:
        copy.start()
    for copy in copies:
        copy.wait()


def load(weights, tables):
    size = sum(w.size * 2 for w in weights)
    arrays = [*weights, *tables]
    out = pl.pallas_call(
        load_kernel,
        in_specs=[whole(pltpu.HBM)] * len(arrays),
        out_specs=[whole()] * len(weights) + [whole(SMEM)] * len(tables),
        out_shape=[pltpu.VMEM(w.shape, w.dtype) for w in weights] + [pltpu.SMEM(t.shape, t.dtype) for t in tables],
        scratch_shapes=[pltpu.SemaphoreType.DMA((len(arrays),))],
        compiler_params=pltpu.CompilerParams(vmem_limit_bytes=2 * MIB),
        cost_estimate=pl.CostEstimate(flops=0, bytes_accessed=2 * size, transcendentals=0),
        name="load",
    )(*[pltpu.with_memory_space_constraint(a, pltpu.HBM) for a in arrays])
    return out[: len(weights)], out[len(weights) :]


def expert_kernel(x_ref, wg_ref, wu_ref, wd_hbm, out_ref, wide_ref, flat_ref, hidden_ref, wd_ref, sem):
    rows, pieces, _ = x_ref.shape
    hidden_width = wg_ref.shape[1]
    width = pieces * LANES
    stride = pieces + GAP
    ncols = 256
    dcols = 1024
    group = 16
    down_copy = pltpu.make_async_copy(wd_hbm, wd_ref, sem)
    down_copy.start()

    def spread(i, carry):
        base = pl.multiple_of(i * group, group)
        for r in range(group):
            wide_ref[pl.ds(r * stride, pieces), :] = x_ref[base + r].astype(F32)
        for s in range(pieces):
            low = wide_ref[pl.ds(s, 8, stride=stride), :]
            high = wide_ref[pl.ds(8 * stride + s, 8, stride=stride), :]
            flat_ref[pl.ds(base, group), pl.ds(s * LANES, LANES)] = jnp.concatenate([low, high], axis=0).astype(BF16)
        return carry

    lax.fori_loop(0, rows // group, spread, 0)

    for n in range(hidden_width // ncols):
        at = pl.ds(n * ncols, ncols)
        gate = jnp.dot(flat_ref[...], wg_ref[:, at], preferred_element_type=F32)
        up = jnp.dot(flat_ref[...], wu_ref[:, at], preferred_element_type=F32)
        hidden_ref[:, at] = (gate / (1.0 + jnp.exp(-gate)) * up).astype(BF16)

    down_copy.wait()
    for n in range(width // dcols):
        done = jnp.dot(hidden_ref[...], wd_ref[:, pl.ds(n * dcols, dcols)], preferred_element_type=F32)
        for r in range(0, rows, 8):
            for s in range(dcols // LANES):
                wide_ref[pl.ds(r * stride + n * (dcols // LANES) + s, 8, stride=stride), :] = done[
                    r : r + 8, s * LANES : (s + 1) * LANES
                ]
        if (n + 1) * dcols * 2 == width:
            for r in range(rows):
                out_ref[r, : pieces // 2] = wide_ref[pl.ds(r * stride, pieces // 2), :].astype(BF16)

    def narrow(i, carry):
        base = pl.multiple_of(i * group, group)
        for r in range(group):
            late = wide_ref[pl.ds((base + r) * stride + pieces // 2, pieces // 2), :]
            out_ref[base + r, pieces // 2 :] = late.astype(BF16)
        return carry

    lax.fori_loop(0, rows // group, narrow, 0)


def expert(x, wg, wu, wd):
    rows, pieces, _ = x.shape
    width, hidden_width = wg.shape
    near = [pltpu.with_memory_space_constraint(w, pltpu.VMEM) for w in (wg, wu)]
    return pl.pallas_call(
        expert_kernel,
        in_specs=[whole()] * 3 + [whole(pltpu.HBM)],
        out_specs=whole(),
        out_shape=jax.ShapeDtypeStruct(x.shape, BF16),
        scratch_shapes=[
            pltpu.VMEM((rows * (pieces + GAP) + SPARE, LANES), F32),
            pltpu.VMEM((rows, width), BF16),
            pltpu.VMEM((rows, hidden_width), BF16),
            pltpu.VMEM(wd.shape, BF16),
            pltpu.SemaphoreType.DMA,
        ],
        compiler_params=pltpu.CompilerParams(vmem_limit_bytes=20 * MIB),
        name="expert",
    )(x, *near, pltpu.with_memory_space_constraint(wd, pltpu.HBM))


def combine_kernel(ids_ref, slots_ref, probs_ref, rows_ref, out_ref, wide_ref):
    rows, width = out_ref.shape
    pieces = width // LANES
    top = ids_ref.shape[0]
    stride = pieces + GAP

    def one(t, carry):
        total = None
        for k in range(top):
            term = rows_ref[ids_ref[k, t], slots_ref[k, t]].astype(F32) * probs_ref[k, t]
            total = term if total is None else total + term
        wide_ref[pl.ds(t * stride, pieces), :] = total
        return carry

    lax.fori_loop(0, rows, one, 0, unroll=True)
    for s in range(pieces):
        low = wide_ref[pl.ds(s, 8, stride=stride), :]
        high = wide_ref[pl.ds(8 * stride + s, 8, stride=stride), :]
        out_ref[:, pl.ds(s * LANES, LANES)] = jnp.concatenate([low, high], axis=0).astype(BF16)


def combine(ids, slots, probs, returned, width):
    rows = ids.shape[1]
    return pl.pallas_call(
        combine_kernel,
        in_specs=[whole(SMEM)] * 3 + [whole()],
        out_specs=whole(),
        out_shape=jax.ShapeDtypeStruct((rows, width), BF16),
        scratch_shapes=[pltpu.VMEM((rows * (width // LANES + GAP) + SPARE, LANES), F32)],
        compiler_params=pltpu.CompilerParams(vmem_limit_bytes=4 * MIB),
        name="combine",
    )(ids, slots, probs, returned)


def on_device(
    queries,
    key_cache,
    value_cache,
    new_keys,
    new_values,
    lengths,
    out_proj,
    residual,
    norm_gain,
    expert_ids,
    expert_slots,
    gate_probs,
    w_gate,
    w_up,
    w_down,
):
    row_count = queries.shape[0]
    width = out_proj.shape[1]
    pieces = width // LANES
    sec_count, group_count = lax.axis_size("sec"), lax.axis_size("kv")
    expert_count = sec_count * lax.axis_size("req") * group_count
    row_share, top_count = expert_ids.shape
    capacity = top_count * row_share // expert_count + 1
    sec = lax.axis_index("sec").astype(jnp.int32).reshape(1)
    kv = lax.axis_index("kv").astype(jnp.int32).reshape(1)

    theirs, mine = attend(
        sec,
        kv,
        lengths.reshape(1, row_count),
        queries,
        key_cache.reshape(-1, LANES),
        value_cache.reshape(-1, LANES),
        new_keys.reshape(row_count, LANES),
        new_values.reshape(row_count, LANES),
        out_proj,
    )

    def other_core(x):
        return lax.ppermute(x, "sec", [(i, 1 - i) for i in range(sec_count)])

    def along(x, step):
        pairs = [
            (c * group_count + i, c * group_count + (i + step * (1 - 2 * c)) % group_count)
            for c in range(sec_count)
            for i in range(group_count)
        ]
        return lax.ppermute(x, ("sec", "kv"), pairs)

    far, before, keep, after = join(mine, other_core(theirs), group_count)
    parts = [keep, along(after, 1), along(before, -1), along(far, 2)]
    weights, tables = load((w_gate[0], w_up[0]), (expert_ids.T, expert_slots.T, gate_probs.T))
    ids, slots, probs = tables
    stream, outgoing = route(ids, slots, parts, residual, norm_gain.reshape(1, width), expert_count, capacity)

    def exchange(rows):
        sent = rows.reshape(expert_count, capacity * pieces, LANES)
        return lax.all_to_all(sent, ("sec", "req", "kv"), split_axis=0, concat_axis=0, tiled=True)

    outgoing, *weights = lax.optimization_barrier((outgoing, *weights))
    arrived = exchange(outgoing).reshape(expert_count * capacity, pieces, LANES)
    finished = expert(arrived, *weights, w_down[0])
    returned = exchange(finished).reshape(expert_count, capacity, pieces, LANES)
    moe_out = combine(ids, slots, probs, returned, width)
    return (stream, moe_out)


def solution(mesh):
    return jax.shard_map(
        on_device,
        mesh=mesh,
        in_specs=(
            P("req", ("kv", "sec")),
            P("req", "kv", None, None),
            P("req", "kv", None, None),
            P("req", "kv", None),
            P("req", "kv", None),
            P("req"),
            P(("kv", "sec"), None),
            P(("req", "sec", "kv"), None),
            P(),
            P(("req", "sec", "kv"), None),
            P(("req", "sec", "kv"), None),
            P(("req", "sec", "kv"), None),
            P(("sec", "req", "kv"), None, None),
            P(("sec", "req", "kv"), None, None),
            P(("sec", "req", "kv"), None, None),
        ),
        out_specs=(P(("req", "sec", "kv"), None), P(("req", "sec", "kv"), None)),
        check_vma=False,
    )
```

```python
import math

import jax
import jax.numpy as jnp
from jax import lax
from jax.experimental import pallas as pl
from jax.experimental.pallas import tpu as pltpu
from jax.sharding import PartitionSpec as P

LANES = 128
F32 = jnp.float32
BF16 = jnp.bfloat16
MIB = 1 << 20

GAP = 1
SPARE = 40

VMEM = pltpu.VMEM
SMEM = pltpu.SMEM


def whole(space=VMEM):
    return pl.BlockSpec(memory_space=space)


BLOCKS = 4


def attend_kernel(
    sec_ref,
    kv_ref,
    len_hbm,
    q_hbm,
    kc_hbm,
    vc_hbm,
    nk_hbm,
    nv_hbm,
    wo_hbm,
    theirs_ref,
    mine_ref,
    len_ref,
    q_ref,
    kc_ref,
    vc_ref,
    nk_ref,
    nv_ref,
    wo_ref,
    attn_ref,
    sems,
):
    rows, head_width = q_ref.shape
    heads = head_width // LANES
    positions = kc_ref.shape[0] // rows
    group = 8
    to_exponent = math.log2(math.e) / LANES**0.5
    half = rows // 2
    far = half // BLOCKS

    small = [
        pltpu.make_async_copy(source, target, sems.at[i])
        for i, (source, target) in enumerate(((len_hbm, len_ref), (q_hbm, q_ref), (nk_hbm, nk_ref), (nv_hbm, nv_ref)))
    ]
    key_copy = pltpu.make_async_copy(kc_hbm, kc_ref, sems.at[4])
    value_copy = pltpu.make_async_copy(vc_hbm, vc_ref, sems.at[5])
    wo_copy = pltpu.make_async_copy(wo_hbm, wo_ref, sems.at[6])
    for copy in (*small, key_copy, value_copy, wo_copy):
        copy.start()

    for copy in small:
        copy.wait()
    r = lax.broadcasted_iota(jnp.int32, (rows, rows), 0)
    c = lax.broadcasted_iota(jnp.int32, (rows, rows), 1)
    lengths = jnp.sum(jnp.where(r == c, len_ref[...], 0).astype(F32), axis=1, keepdims=True)
    span = group * positions
    row_token = lax.broadcasted_iota(jnp.int32, (heads * group, span), 0) % group
    column = lax.broadcasted_iota(jnp.int32, (heads * group, span), 1)
    own_column = column - row_token * positions
    own_position = jnp.where(own_column >= 0, own_column, positions).astype(F32)

    def per_head(rows_of_group):
        return jnp.concatenate([rows_of_group] * heads, axis=0)

    def group_rows(ref, g):
        pair = ref[pl.ds(g // 2 * 2 * group, 2 * group), :].astype(F32)
        return pair[g % 2 * group : (g % 2 + 1) * group]

    groups = rows // group
    scores, own_scores, raised, own_raised, outs = [], [], [], [], []
    key_copy.wait()
    for g in range(groups):
        q_rows = group_rows(q_ref, g)
        q = jnp.concatenate([q_rows[:, h * LANES : (h + 1) * LANES] for h in range(heads)], axis=0)
        keys = kc_ref[pl.ds(g * span, span), :]
        score = lax.dot_general(q.astype(BF16), keys, (((1,), (1,)), ((), ())), preferred_element_type=F32)
        scores.append(jnp.where(own_position < per_head(lengths[g * group : (g + 1) * group]), score, -jnp.inf))
        own_scores.append(jnp.sum(q * per_head(group_rows(nk_ref, g)), axis=1, keepdims=True))
    for score, own_score in zip(scores, own_scores):
        highest = jnp.maximum(jnp.max(score, axis=1, keepdims=True), own_score)
        raised.append(jnp.exp2((score - highest) * to_exponent))
        own_raised.append(jnp.exp2((own_score - highest) * to_exponent))
    value_copy.wait()
    for g in range(groups):
        inverse = 1.0 / (jnp.sum(raised[g], axis=1, keepdims=True) + own_raised[g])
        values = vc_ref[pl.ds(g * span, span), :]
        out = jnp.dot(raised[g].astype(BF16), values, preferred_element_type=F32)
        outs.append((out + own_raised[g] * per_head(group_rows(nv_ref, g))) * inverse)
    for g in range(0, groups, 2):
        block, blocks = g * group // far, half // far
        way = 1 - 2 * (block // blocks)
        turned = lax.rem(way * (block % blocks - kv_ref[0]) + blocks + blocks // 2, blocks)
        side = lax.rem(block // blocks + 1 - sec_ref[0], 2)
        place = pl.multiple_of(side * half + turned * far, 2 * group)
        for h in range(heads):
            pair = [outs[g + j][h * group : (h + 1) * group] for j in range(2)]
            attn_ref[pl.ds(place, 2 * group), pl.ds(h * LANES, LANES)] = jnp.concatenate(pair, axis=0).astype(BF16)

    wo_copy.wait()
    proj = jnp.dot(attn_ref[...], wo_ref[...], preferred_element_type=F32)
    theirs_ref[...] = proj[:half].astype(BF16)
    mine_ref[...] = proj[half:].astype(BF16)


def attend(sec, kv, lengths, q, kc, vc, nk, nv, wo):
    rows, head_width = q.shape
    width = wo.shape[1]
    out = [jax.ShapeDtypeStruct((rows // 2, width), BF16)]
    far = [pltpu.with_memory_space_constraint(a, pltpu.HBM) for a in (lengths, q, kc, vc, nk, nv, wo)]
    return pl.pallas_call(
        attend_kernel,
        in_specs=[whole(SMEM)] * 2 + [whole(pltpu.HBM)] * 7,
        out_specs=[whole()] * 2,
        out_shape=out * 2,
        scratch_shapes=[pltpu.VMEM(a.shape, a.dtype) for a in (lengths, q, kc, vc, nk, nv)]
        + [
            pltpu.VMEM(wo.shape, BF16),
            pltpu.VMEM((rows, head_width), BF16),
            pltpu.SemaphoreType.DMA((7,)),
        ],
        compiler_params=pltpu.CompilerParams(vmem_limit_bytes=14 * MIB),
        name="attend",
    )(sec, kv, *far)


def join_kernel(mine_ref, got_ref, *out_refs):
    rows = out_refs[0].shape[0]
    for i, out_ref in enumerate(out_refs):
        at = pl.ds(i * rows, rows)
        out_ref[...] = (mine_ref[at, :].astype(F32) + got_ref[at, :].astype(F32)).astype(BF16)


def join(mine, got, parts):
    rows, width = mine.shape
    out = jax.ShapeDtypeStruct((rows // parts, width), BF16)
    return pl.pallas_call(
        join_kernel,
        in_specs=[whole(), whole()],
        out_specs=[whole()] * parts,
        out_shape=[out] * parts,
        compiler_params=pltpu.CompilerParams(vmem_limit_bytes=4 * MIB),
        name="join",
    )(mine, got)


def route_kernel(ids_ref, slots_ref, *refs):
    part_refs, (residual_ref, gain_ref, stream_hbm, out_ref, wide_ref, stream_ref, sem) = refs[:-7], refs[-7:]
    rows, width = residual_ref.shape
    pieces = width // LANES
    top = ids_ref.shape[0]
    stride = pieces + GAP
    out_ref[...] = jnp.zeros_like(out_ref)
    proj = part_refs[0][...].astype(F32)
    for part_ref in part_refs[1:]:
        proj = proj + part_ref[...].astype(F32)
    stream = (residual_ref[...].astype(F32) + proj).astype(BF16)
    stream_ref[...] = stream
    leave = pltpu.make_async_copy(stream_ref, stream_hbm, sem)
    leave.start()
    widened = stream.astype(F32)
    mean_square = jnp.mean(widened * widened, axis=-1, keepdims=True)
    normed = widened * lax.rsqrt(mean_square + 1e-06) * gain_ref[...]
    for t in range(0, rows, 8):
        for s in range(pieces):
            wide_ref[pl.ds(t * stride + s, 8, stride=stride), :] = normed[t : t + 8, s * LANES : (s + 1) * LANES]

    def one(t, carry):
        row = wide_ref[pl.ds(t * stride, pieces), :].astype(BF16)
        for k in range(top):
            out_ref[ids_ref[k, t], slots_ref[k, t]] = row
        return carry

    lax.fori_loop(0, rows, one, 0, unroll=4)
    leave.wait()


def route(ids, slots, parts, residual, gain, expert_count, capacity):
    rows, width = residual.shape
    pieces = width // LANES
    return pl.pallas_call(
        route_kernel,
        in_specs=[whole(SMEM), whole(SMEM)] + [whole()] * (len(parts) + 2),
        out_specs=[whole(pl.ANY), whole()],
        out_shape=[
            jax.ShapeDtypeStruct((rows, width), BF16),
            jax.ShapeDtypeStruct((expert_count, capacity, pieces, LANES), BF16),
        ],
        scratch_shapes=[
            pltpu.VMEM((rows * (pieces + GAP) + SPARE, LANES), F32),
            pltpu.VMEM((rows, width), BF16),
            pltpu.SemaphoreType.DMA,
        ],
        compiler_params=pltpu.CompilerParams(vmem_limit_bytes=4 * MIB),
        name="route",
    )(ids, slots, *parts, residual, gain)


def load_kernel(*refs):
    count = len(refs) // 2
    sems = refs[-1]
    copies = [pltpu.make_async_copy(refs[i], refs[count + i], sems.at[i]) for i in range(count)]
    for copy in copies:
        copy.start()
    for copy in copies:
        copy.wait()


def load(weights, tables):
    size = sum(w.size * 2 for w in weights)
    arrays = [*weights, *tables]
    out = pl.pallas_call(
        load_kernel,
        in_specs=[whole(pltpu.HBM)] * len(arrays),
        out_specs=[whole()] * len(weights) + [whole(SMEM)] * len(tables),
        out_shape=[pltpu.VMEM(w.shape, w.dtype) for w in weights] + [pltpu.SMEM(t.shape, t.dtype) for t in tables],
        scratch_shapes=[pltpu.SemaphoreType.DMA((len(arrays),))],
        compiler_params=pltpu.CompilerParams(vmem_limit_bytes=2 * MIB),
        cost_estimate=pl.CostEstimate(flops=0, bytes_accessed=2 * size, transcendentals=0),
        name="load",
    )(*[pltpu.with_memory_space_constraint(a, pltpu.HBM) for a in arrays])
    return out[: len(weights)], out[len(weights) :]


def expert_kernel(x_ref, wg_ref, wu_ref, wd_hbm, out_ref, wide_ref, flat_ref, hidden_ref, wd_ref, sem):
    rows, pieces, _ = x_ref.shape
    hidden_width = wg_ref.shape[1]
    width = pieces * LANES
    stride = pieces + GAP
    ncols = 256
    dcols = 1024
    group = 16
    down_copy = pltpu.make_async_copy(wd_hbm, wd_ref, sem)
    down_copy.start()

    def spread(i, carry):
        base = pl.multiple_of(i * group, group)
        for r in range(group):
            wide_ref[pl.ds(r * stride, pieces), :] = x_ref[base + r].astype(F32)
        for s in range(pieces):
            low = wide_ref[pl.ds(s, 8, stride=stride), :]
            high = wide_ref[pl.ds(8 * stride + s, 8, stride=stride), :]
            flat_ref[pl.ds(base, group), pl.ds(s * LANES, LANES)] = jnp.concatenate([low, high], axis=0).astype(BF16)
        return carry

    lax.fori_loop(0, rows // group, spread, 0)

    for n in range(hidden_width // ncols):
        at = pl.ds(n * ncols, ncols)
        gate = jnp.dot(flat_ref[...], wg_ref[:, at], preferred_element_type=F32)
        up = jnp.dot(flat_ref[...], wu_ref[:, at], preferred_element_type=F32)
        hidden_ref[:, at] = (0.5 * gate * (1.0 + jnp.tanh(0.5 * gate)) * up).astype(BF16)

    down_copy.wait()
    for n in range(width // dcols):
        done = jnp.dot(hidden_ref[...], wd_ref[:, pl.ds(n * dcols, dcols)], preferred_element_type=F32)
        for r in range(0, rows, 8):
            for s in range(dcols // LANES):
                wide_ref[pl.ds(r * stride + n * (dcols // LANES) + s, 8, stride=stride), :] = done[
                    r : r + 8, s * LANES : (s + 1) * LANES
                ]
        if (n + 1) * dcols * 2 == width:
            for r in range(rows):
                out_ref[r, : pieces // 2] = wide_ref[pl.ds(r * stride, pieces // 2), :].astype(BF16)

    def narrow(i, carry):
        base = pl.multiple_of(i * group, group)
        for r in range(group):
            late = wide_ref[pl.ds((base + r) * stride + pieces // 2, pieces // 2), :]
            out_ref[base + r, pieces // 2 :] = late.astype(BF16)
        return carry

    lax.fori_loop(0, rows // group, narrow, 0)


def expert(x, wg, wu, wd):
    rows, pieces, _ = x.shape
    width, hidden_width = wg.shape
    near = [pltpu.with_memory_space_constraint(w, pltpu.VMEM) for w in (wg, wu)]
    return pl.pallas_call(
        expert_kernel,
        in_specs=[whole()] * 3 + [whole(pltpu.HBM)],
        out_specs=whole(),
        out_shape=jax.ShapeDtypeStruct(x.shape, BF16),
        scratch_shapes=[
            pltpu.VMEM((rows * (pieces + GAP) + SPARE, LANES), F32),
            pltpu.VMEM((rows, width), BF16),
            pltpu.VMEM((rows, hidden_width), BF16),
            pltpu.VMEM(wd.shape, BF16),
            pltpu.SemaphoreType.DMA,
        ],
        compiler_params=pltpu.CompilerParams(vmem_limit_bytes=20 * MIB),
        name="expert",
    )(x, *near, pltpu.with_memory_space_constraint(wd, pltpu.HBM))


def combine_kernel(ids_ref, slots_ref, probs_ref, rows_ref, out_ref, wide_ref):
    rows, width = out_ref.shape
    pieces = width // LANES
    top = ids_ref.shape[0]
    stride = pieces + GAP

    def one(t, carry):
        total = None
        for k in range(top):
            term = rows_ref[ids_ref[k, t], slots_ref[k, t]].astype(F32) * probs_ref[k, t]
            total = term if total is None else total + term
        wide_ref[pl.ds(t * stride, pieces), :] = total
        return carry

    lax.fori_loop(0, rows, one, 0, unroll=True)
    for s in range(pieces):
        low = wide_ref[pl.ds(s, 8, stride=stride), :]
        high = wide_ref[pl.ds(8 * stride + s, 8, stride=stride), :]
        out_ref[:, pl.ds(s * LANES, LANES)] = jnp.concatenate([low, high], axis=0).astype(BF16)


def combine(ids, slots, probs, returned, width):
    rows = ids.shape[1]
    return pl.pallas_call(
        combine_kernel,
        in_specs=[whole(SMEM)] * 3 + [whole()],
        out_specs=whole(),
        out_shape=jax.ShapeDtypeStruct((rows, width), BF16),
        scratch_shapes=[pltpu.VMEM((rows * (width // LANES + GAP) + SPARE, LANES), F32)],
        compiler_params=pltpu.CompilerParams(vmem_limit_bytes=4 * MIB),
        name="combine",
    )(ids, slots, probs, returned)


def on_device(
    queries,
    key_cache,
    value_cache,
    new_keys,
    new_values,
    lengths,
    out_proj,
    residual,
    norm_gain,
    expert_ids,
    expert_slots,
    gate_probs,
    w_gate,
    w_up,
    w_down,
):
    row_count = queries.shape[0]
    width = out_proj.shape[1]
    pieces = width // LANES
    sec_count, group_count = lax.axis_size("sec"), lax.axis_size("kv")
    expert_count = sec_count * lax.axis_size("req") * group_count
    row_share, top_count = expert_ids.shape
    capacity = top_count * row_share // expert_count + 1
    sec = lax.axis_index("sec").astype(jnp.int32).reshape(1)
    kv = lax.axis_index("kv").astype(jnp.int32).reshape(1)

    theirs, mine = attend(
        sec,
        kv,
        lengths.reshape(1, row_count),
        queries,
        key_cache.reshape(-1, LANES),
        value_cache.reshape(-1, LANES),
        new_keys.reshape(row_count, LANES),
        new_values.reshape(row_count, LANES),
        out_proj,
    )

    def other_core(x):
        return lax.ppermute(x, "sec", [(i, 1 - i) for i in range(sec_count)])

    def along(x, step):
        pairs = [
            (c * group_count + i, c * group_count + (i + step * (1 - 2 * c)) % group_count)
            for c in range(sec_count)
            for i in range(group_count)
        ]
        return lax.ppermute(x, ("sec", "kv"), pairs)

    far, before, keep, after = join(mine, other_core(theirs), group_count)
    parts = [keep, along(after, 1), along(before, -1), along(far, 2)]
    weights, tables = load((w_gate[0], w_up[0]), (expert_ids.T, expert_slots.T, gate_probs.T))
    ids, slots, probs = tables
    stream, outgoing = route(ids, slots, parts, residual, norm_gain.reshape(1, width), expert_count, capacity)

    def exchange(rows):
        sent = rows.reshape(expert_count, capacity * pieces, LANES)
        return lax.all_to_all(sent, ("sec", "req", "kv"), split_axis=0, concat_axis=0, tiled=True)

    outgoing, *weights = lax.optimization_barrier((outgoing, *weights))
    arrived = exchange(outgoing).reshape(expert_count * capacity, pieces, LANES)
    finished = expert(arrived, *weights, w_down[0])
    returned = exchange(finished).reshape(expert_count, capacity, pieces, LANES)
    moe_out = combine(ids, slots, probs, returned, width)
    return (stream, moe_out)


def solution(mesh):
    return jax.shard_map(
        on_device,
        mesh=mesh,
        in_specs=(
            P("req", ("kv", "sec")),
            P("req", "kv", None, None),
            P("req", "kv", None, None),
            P("req", "kv", None),
            P("req", "kv", None),
            P("req"),
            P(("kv", "sec"), None),
            P(("req", "sec", "kv"), None),
            P(),
            P(("req", "sec", "kv"), None),
            P(("req", "sec", "kv"), None),
            P(("req", "sec", "kv"), None),
            P(("sec", "req", "kv"), None, None),
            P(("sec", "req", "kv"), None, None),
            P(("sec", "req", "kv"), None, None),
        ),
        out_specs=(P(("req", "sec", "kv"), None), P(("req", "sec", "kv"), None)),
        check_vma=False,
    )
```
